256 devices in a mesh: rep: 4 (over y), ep: 64 (over z, x, core).
Axes of the slice: x: 4, y: 4, z: 8, core: 2. Of those that a mesh axis runs over, the one named last changes fastest.
Arguments:
- tokens: bfloat16 [8192, 4096], P(('rep', 'ep')), parts along dimension 0, may hold values from -170 to 170
- norm_gain: float32 [4096], replicated, may hold values from 0.1 to 1.9
- gate_weight: bfloat16 [256, 4096, 768], P(('rep', 'ep')), parts along dimension 0, may hold values from -0.09375 to 0.09375
- up_weight: bfloat16 [256, 4096, 768], P(('rep', 'ep')), parts along dimension 0, may hold values from -0.09375 to 0.09375
- route_ids: int32 [8192, 8], P(('rep', 'ep')), parts along dimension 0, may hold values from 0 to 63, all different within a row; in each aligned block of 32 rows (0 to 31, 32 to 63, ...) at most 8 rows name the same one
- route_scores: float32 [8192, 8], P(('rep', 'ep')), parts along dimension 0, may hold values from 0.1 to 1
- queries: bfloat16 [8192, 4096], P(('rep', 'ep')), parts along dimension 0, may hold values from -500 to 500
- key_cache: bfloat16 [8192, 16, 256], P(('rep', 'ep')), parts along dimension 0, may hold values from -7 to 7
- value_cache: bfloat16 [8192, 16, 256], P(('rep', 'ep')), parts along dimension 0, may hold values from -6 to 6
- new_keys: bfloat16 [8192, 256], P(('rep', 'ep')), parts along dimension 0, may hold values from -6 to 6
- new_values: bfloat16 [8192, 256], P(('rep', 'ep')), parts along dimension 0, may hold values from -6 to 6
- cache_lengths: int32 [8192], P(('rep', 'ep')), parts along dimension 0, may hold values from 2 to 16, as said below
Outputs:
- expert_terms: bfloat16 [8192, 8, 768], P(('rep', 'ep')), parts along dimension 0
- attended: bfloat16 [8192, 4096], P(('rep', 'ep')), parts along dimension 0
The draws below stay inside these ranges and needn't reach their ends.
There are 4 independent parts, one for each index of `rep`. The reference program is written for one: setup_inputs(seed, part) draws one part's arguments, and reference() takes and returns one part's arrays. A program takes and returns all parts, laid end to end along the dimension named above; an argument that names none is the same for every part. Nothing has to cross between parts.
Inputs may be any that keep to these rules, and one draw needn't show every extreme that they name: `route_ids`: each row names 8 different experts; among the rows of one device no expert is named more than 8 times, a bound that some block reaches. `cache_lengths`: some row has exactly 16.
All inputs are finite; a program needn't handle non-finite values.
Results may differ from the reference program's by a relative error of at most 0.02.
Values may be sent and summed in bfloat16 or wider, within the bound.
A program may use at most 128 MiB of HBM per device.

```python
import math
import jax
import jax.numpy as jnp
import numpy as np
from jax import lax

D = 4096
FFW = 768
QH = 32
KVH = 2
HD = 128
TOPK = 8
TOK_DEV = 32
CACHE = 16
EXPERTS = 64
TOKENS = 2048
MOST = 8
N_EP = 64


def key_base(key):
    return jnp.clip(jax.random.normal(jax.random.fold_in(key, 11), (TOKENS, CACHE, KVH * HD), jnp.float32), -4.0, 4.0)


def draw_tokens(key, part):
    key = jax.random.fold_in(key, 5)
    first_key, second_key, third_key = jax.random.split(key, 3)
    row_scale = jnp.exp(jax.random.uniform(first_key, (TOKENS, 1), jnp.float32, 0.0, math.log(10.0)))
    col_scale = jnp.exp(jax.random.uniform(second_key, (1, D), jnp.float32, 0.0, math.log(10.0)))
    noise = jnp.clip(jax.random.normal(third_key, (TOKENS, D), jnp.float32), -5.0, 5.0)
    return (noise * row_scale * col_scale / 3.0).astype(jnp.bfloat16)


def draw_queries(key, part):
    key = jax.random.fold_in(key, 4)
    query_vals = jnp.clip(jax.random.normal(key, (TOKENS, QH * HD), jnp.float32), -5.0, 5.0)
    return query_vals.astype(jnp.bfloat16)


def draw_key_cache(key, part):
    shared = key_base(key)
    shaped = shared
    return shaped.astype(jnp.bfloat16)


def draw_cache_lengths(key, part):
    key = jax.random.fold_in(key, 9)
    first_key, second_key = jax.random.split(key)
    lengths = jax.random.randint(first_key, (TOKENS,), 2, CACHE + 1)
    filled_row = jax.random.randint(second_key, (), 0, TOKENS)
    return jnp.where(jnp.arange(TOKENS, dtype=jnp.int32) == filled_row, CACHE, lengths).astype(jnp.int32)


def block_levels(own_key, extent, shards, smallest, largest):
    loudness, own = 1.0, jax.random.fold_in(own_key, 6)
    for dim, blocks in shards:
        heights = jnp.exp(jax.random.uniform(jax.random.fold_in(own, dim), (blocks,), jnp.float32, smallest / len(shards), largest / len(shards)))
        loudness = loudness * jnp.repeat(heights, extent[dim] // blocks).reshape([-1 if axis == dim else 1 for axis in range(len(extent))])
    return loudness


def assign_block(key, own, number, rows, amount, top, limit, skew):
    ranking = jax.random.permutation(key, amount)
    packed, usual = portions_of(amount, rows * top, limit, skew, True), portions_of(amount, rows * top, limit, skew, False)
    places = jnp.arange(amount)

    def named(sizes, rotation):
        used = int((sizes > 0).sum())
        fixed = max(1, used // 4)
        moved = fixed + (places - fixed + rotation * (used - fixed)) % max(1, amount - fixed)
        return jnp.zeros((amount,), jnp.int32).at[ranking[jnp.where(places < fixed, places, moved)]].set(jnp.asarray(sizes, jnp.int32))

    sizes = jnp.where(number % 4 == 0, named(packed, number // 4), named(usual, number - number // 4 - 1))
    mixed = jax.random.permutation(jax.random.fold_in(own, 3), amount)
    giver, sink = mixed[0:amount // 2 * 2:2], mixed[1:amount // 2 * 2:2]
    slack = jnp.minimum(sizes[giver] - 1, limit - sizes[sink]) // 2
    slack = jnp.where((giver == ranking[0]) | (sink == ranking[0]) | (sizes[sink] == 0), 0, jnp.maximum(slack, 0))
    moved = jax.random.randint(jax.random.fold_in(own, 4), (amount // 2,), 0, 1 << 20) % (slack + 1)
    sizes = sizes.at[giver].add(-moved).at[sink].add(moved)
    members = jnp.searchsorted(jnp.cumsum(sizes), jnp.arange(rows * top), side="right").astype(jnp.int32)
    listing = members.reshape(top, rows).T
    listing = listing[jax.random.permutation(jax.random.fold_in(own, 1), rows)]
    rotation = jax.random.randint(jax.random.fold_in(own, 2), (rows, 1), 0, top)
    return jnp.take_along_axis(listing, (jnp.arange(top)[None, :] + rotation) % top, axis=1)


def portions_of(amount, total, bound, slope, full):
    loads = [(1 << 20) // math.isqrt(grade ** slope) + 1 for grade in range(1, amount + 1)]
    largest = bound if full else min(bound, max(-(-total // amount), total * loads[0] // sum(loads)))
    least = 1 if total - largest >= amount - 1 else 0
    counts, surplus = [largest] + [least] * (amount - 1), total - largest - least * (amount - 1)
    while surplus > 0:
        movable = [i for i in range(1, amount) if counts[i] < largest] or [i for i in range(1, amount) if counts[i] < bound]
        whole, left = sum([loads[i] for i in movable]), surplus
        for i in movable:
            more = min(bound - counts[i], max(1, left * loads[i] // whole), surplus)
            counts[i] = counts[i] + more
            surplus = surplus - more
    return np.array(counts)


def bell_draw(stream_key, extent, deviation, limit, cuts=(), held_as=jnp.bfloat16):
    level = block_levels(stream_key, extent, cuts, -0.22, 0.18) if cuts else 1.0
    result = jax.random.normal(stream_key, extent, jnp.float32) * deviation * level
    return jnp.minimum(jnp.maximum(result, -limit), limit).astype(held_as)


def setup_inputs(seed: int = 0, part: int = 0) -> dict:
    arg_keys = jax.random.split(jax.random.key(seed), 13)
    own_keys = jax.random.split(jax.random.fold_in(arg_keys[12], part), 13)
    tokens = draw_tokens(jax.random.fold_in(jax.random.fold_in(arg_keys[12], part), 71), part)
    norm_gain = jnp.clip(1.0 + 0.18 * jax.random.normal(arg_keys[1], (D,), jnp.float32), 0.1, 1.9)
    gate_weight = bell_draw(own_keys[2], (EXPERTS, D, FFW), D ** -0.5, 0.09375, ((0, 64),))
    up_weight = bell_draw(own_keys[3], (EXPERTS, D, FFW), D ** -0.5, 0.09375, ((0, 64),))
    route_ids_keys = jax.random.split(jax.random.fold_in(own_keys[4], 1), TOKENS // TOK_DEV)
    route_ids_turns = jax.random.permutation(jax.random.fold_in(own_keys[4], 3), TOKENS // TOK_DEV)
    route_ids = jax.vmap(lambda own, number: assign_block(jax.random.fold_in(own_keys[4], 2), own, number, TOK_DEV, EXPERTS, TOPK, MOST, 2))(route_ids_keys, route_ids_turns).reshape((TOKENS, TOPK))
    route_scores = jnp.clip(jnp.exp(math.log(1.0) - 2.3025851 * jax.random.uniform(own_keys[5], (TOKENS, TOPK), jnp.float32) ** block_levels(own_keys[5], (TOKENS, TOPK), ((0, 64),), -0.2, 0.2)), 0.1, 1.0)
    queries = draw_queries(jax.random.fold_in(jax.random.fold_in(arg_keys[12], part), 71), part)
    key_cache = draw_key_cache(jax.random.fold_in(jax.random.fold_in(arg_keys[12], part), 71), part)
    value_cache = bell_draw(own_keys[8], (TOKENS, CACHE, KVH * HD), 1.0, 6.0, ((0, 64),))
    new_keys = bell_draw(own_keys[9], (TOKENS, KVH * HD), 1.0, 6.0, ((0, 64),))
    new_values = bell_draw(own_keys[10], (TOKENS, KVH * HD), 1.0, 6.0, ((0, 64),))
    cache_lengths = draw_cache_lengths(jax.random.fold_in(jax.random.fold_in(arg_keys[12], part), 71), part)
    return dict(tokens=tokens, norm_gain=norm_gain, gate_weight=gate_weight, up_weight=up_weight, route_ids=route_ids, route_scores=route_scores, queries=queries, key_cache=key_cache, value_cache=value_cache, new_keys=new_keys, new_values=new_values, cache_lengths=cache_lengths)


def rms_rows(hidden, norm_gain):
    values = hidden.astype(jnp.float32)
    mean_sq = lax.optimization_barrier(jnp.mean(values * values, axis=-1, keepdims=True))
    return (values * lax.rsqrt(mean_sq + 1e-06) * norm_gain).astype(jnp.bfloat16)

def attend_rows(queries, key_cache, value_cache, new_keys, new_values, cache_lengths):
    row_count = key_cache.shape[0]
    cache_len = key_cache.shape[1]
    kv_heads = new_keys.shape[1] // HD
    group_size = queries.shape[1] // new_keys.shape[1]
    query_heads = queries.astype(jnp.float32).reshape(row_count, kv_heads, group_size, HD)
    key_heads = key_cache.astype(jnp.float32).reshape(row_count, cache_len, kv_heads, HD)
    value_heads = value_cache.astype(jnp.float32).reshape(row_count, cache_len, kv_heads, HD)
    factor = HD ** (-0.5)
    scores = jnp.einsum('tkgd,tckd->tkgc', query_heads, key_heads) * factor
    own_score = jnp.einsum('tkgd,tkd->tkg', query_heads, new_keys.astype(jnp.float32).reshape(row_count, kv_heads, HD)) * factor
    live_mask = (jnp.arange(cache_len, dtype=jnp.int32)[None, :] < cache_lengths[:, None])[:, None, None, :]
    scores = jnp.where(live_mask, scores, -1e+30)
    top_score = jnp.maximum(lax.optimization_barrier(jnp.max(scores, axis=-1)), own_score)
    weights = jnp.where(live_mask, jnp.exp(scores - top_score[..., None]), 0.0)
    own_weight = jnp.exp(own_score - top_score)
    total_mass = lax.optimization_barrier(jnp.sum(weights, axis=-1)) + own_weight
    prob_bf = (weights / total_mass[..., None]).astype(jnp.bfloat16)
    own_prob = (own_weight / total_mass).astype(jnp.bfloat16)
    attn_sum = jnp.einsum('tkgc,tckd->tkgd', prob_bf.astype(jnp.float32), value_heads)
    fresh = new_values.astype(jnp.float32).reshape(row_count, kv_heads, 1, HD)
    attn_sum = attn_sum + own_prob.astype(jnp.float32)[..., None] * fresh
    return attn_sum.reshape(row_count, -1).astype(jnp.bfloat16)

def reference(tokens, norm_gain, gate_weight, up_weight, route_ids, route_scores, queries, key_cache, value_cache, new_keys, new_values, cache_lengths):
    attended = attend_rows(queries, key_cache, value_cache, new_keys, new_values, cache_lengths)
    hidden = (tokens.astype(jnp.float32) + attended.astype(jnp.float32)).astype(jnp.bfloat16)
    normed = rms_rows(hidden, norm_gain)
    positions = jnp.arange(TOKENS, dtype=jnp.int32)
    capacity = N_EP * MOST

    def one_expert(carried, expert):
        hit_mask = jnp.any(route_ids == expert, axis=1)
        ordering = jnp.argsort(jnp.where(hit_mask, positions, positions + TOKENS))[:capacity].astype(jnp.int32)
        chosen = normed[ordering]
        gate_val = jnp.dot(chosen, gate_weight[expert], preferred_element_type=jnp.float32)
        up_val = jnp.dot(chosen, up_weight[expert], preferred_element_type=jnp.float32)
        activation = (jax.nn.silu(gate_val) * up_val).astype(jnp.bfloat16)
        usable = hit_mask[ordering]
        per_token = jnp.zeros((TOKENS, FFW), jnp.float32).at[ordering].set(jnp.where(usable[:, None], activation.astype(jnp.float32), 0.0))
        carried = carried + jnp.where((route_ids == expert)[:, :, None], per_token[:, None, :], 0.0)
        return (carried, None)
    picked, _ = lax.scan(one_expert, jnp.zeros((TOKENS, TOPK, FFW), jnp.float32), jnp.arange(EXPERTS, dtype=jnp.int32))
    route_share = route_scores / lax.optimization_barrier(jnp.sum(route_scores, axis=1, keepdims=True))
    expert_terms = (route_share[:, :, None] * picked).astype(jnp.bfloat16)
    return (expert_terms, attended)
```

```python
import jax
import jax.experimental.pallas as pl
import jax.experimental.pallas.tpu as pltpu
import jax.numpy as jnp
from jax import lax
from jax.sharding import PartitionSpec as P

HD = 128
D = 4096
FFW = 768
TOK = 32
CAP = 8
NZ = 8
PLANE = 8
META = 128
HALF = D // 2
MESH = pl.DeviceIdType.MESH


def rms_rows(hidden, norm_gain):
    values = hidden.astype(jnp.float32)
    mean_sq = jnp.mean(values * values, axis=-1, keepdims=True)
    return (values * lax.rsqrt(mean_sq + 1e-06) * norm_gain).astype(jnp.bfloat16)


def attend_rows(queries, key_cache, value_cache, new_keys, new_values, cache_lengths):
    row_count = key_cache.shape[0]
    cache_len = key_cache.shape[1]
    kv_heads = new_keys.shape[1] // HD
    group_size = queries.shape[1] // new_keys.shape[1]
    query_heads = queries.reshape(row_count, kv_heads, group_size, HD)
    key_heads = key_cache.reshape(row_count, cache_len, kv_heads, HD)
    value_heads = value_cache.reshape(row_count, cache_len, kv_heads, HD)
    factor = HD ** (-0.5)
    scores = (
        jnp.einsum("tkgd,tckd->tkgc", query_heads, key_heads, preferred_element_type=jnp.float32)
        * factor
    )
    own_score = (
        jnp.einsum(
            "tkgd,tkd->tkg",
            query_heads,
            new_keys.reshape(row_count, kv_heads, HD),
            preferred_element_type=jnp.float32,
        )
        * factor
    )
    live_mask = (jnp.arange(cache_len, dtype=jnp.int32)[None, :] < cache_lengths[:, None])[
        :, None, None, :
    ]
    scores = jnp.where(live_mask, scores, -1e30)
    top_score = jnp.maximum(jnp.max(scores, axis=-1), own_score)
    weights = jnp.where(live_mask, jnp.exp(scores - top_score[..., None]), 0.0)
    own_weight = jnp.exp(own_score - top_score)
    total_mass = jnp.sum(weights, axis=-1) + own_weight
    prob_bf = (weights / total_mass[..., None]).astype(jnp.bfloat16)
    own_prob = (own_weight / total_mass).astype(jnp.bfloat16)
    attn_sum = jnp.einsum(
        "tkgc,tckd->tkgd", prob_bf, value_heads, preferred_element_type=jnp.float32
    )
    fresh = new_values.astype(jnp.float32).reshape(row_count, kv_heads, 1, HD)
    attn_sum = attn_sum + own_prob.astype(jnp.float32)[..., None] * fresh
    return attn_sum.reshape(row_count, -1).astype(jnp.bfloat16)


def layer_kernel(
    rows_ref, gate_hbm, up_hbm, pos_ref, share_ref, out_ref,
    raw, half_out, pair_out, half_in, pair_in, gate_w, up_w, act, ret_out, ret_in,
    w_sem, z_send, z_recv, p_send, p_recv, r_send, r_recv,
):
    ep = lax.axis_index("ep")
    z = ep // PLANE
    spot = ep % PLANE

    def at_z(dz):
        return (z + dz + NZ) % NZ

    def dev(zz, ss):
        return {"ep": zz * PLANE + ss}

    w_copies = [
        pltpu.make_async_copy(gate_hbm.at[0], gate_w, w_sem.at[0]),
        pltpu.make_async_copy(up_hbm.at[0], up_w, w_sem.at[1]),
    ]
    for copy in w_copies:
        copy.start()
    barrier = pltpu.get_barrier_semaphore()

    def greet(o, carry):
        pl.semaphore_signal(
            barrier, inc=1, device_id={"ep": (ep + o) % (NZ * PLANE)}, device_id_type=MESH
        )
        return carry

    lax.fori_loop(1, NZ * PLANE, greet, 0)
    raw[z] = rows_ref[...]
    pl.semaphore_wait(barrier, NZ * PLANE - 1)

    def hop(sign, k):
        block = raw.at[at_z(-sign * (k - 1))]
        if k == 4:
            block = block.at[pl.ds(0 if sign > 0 else 16, 16)]
        idx = (k - 1) + (0 if sign > 0 else 4)
        return pltpu.make_async_remote_copy(
            src_ref=block,
            dst_ref=block,
            send_sem=z_send.at[idx],
            recv_sem=z_recv.at[idx],
            device_id=dev(at_z(sign), spot),
            device_id_type=MESH,
        )

    def arrived(sign, k):
        block = raw.at[at_z(-sign * k)]
        if k == 4:
            block = block.at[pl.ds(0 if sign > 0 else 16, 16)]
        idx = (k - 1) + (0 if sign > 0 else 4)
        pltpu.make_async_remote_copy(
            src_ref=block,
            dst_ref=block,
            send_sem=z_send.at[idx],
            recv_sem=z_recv.at[idx],
            device_id=dev(at_z(sign), spot),
            device_id_type=MESH,
        ).wait_recv()

    slot_row = lax.broadcasted_iota(jnp.int32, (PLANE * CAP, META), 0)
    lane = lax.broadcasted_iota(jnp.int32, (PLANE * CAP, META), 1)
    expert_hot = (lane == z * PLANE + slot_row // CAP).astype(jnp.bfloat16)
    wanted = (
        lax.broadcasted_iota(jnp.int32, (PLANE * CAP, TOK), 0) % CAP
    ).astype(jnp.float32)

    def placing(zz):
        meta = raw[zz, :, D:]
        ranks = lax.dot_general(
            expert_hot, meta, (((1,), (1,)), ((), ())), preferred_element_type=jnp.float32
        )
        return (ranks == wanted).astype(jnp.float32).astype(jnp.bfloat16)

    def slots(place, zz, lo, width):
        got = jnp.dot(place, raw[zz, :, lo : lo + width], preferred_element_type=jnp.float32)
        return got.reshape(PLANE, CAP, width)

    def compact_half(i, zz):
        place = placing(zz)
        for lo in range(0, HALF, 1024):
            both = jnp.concatenate(
                [slots(place, zz, lo, 1024), slots(place, zz, HALF + lo, 1024)], axis=1
            )
            half_out[i, :, :, lo : lo + 1024] = both.astype(jnp.bfloat16)

    def compact_pair(k):
        upper, lower = at_z(k), at_z(-k)
        place_u, place_l = placing(upper), placing(lower)
        for lo in range(0, D, 1024):
            both = jnp.concatenate(
                [slots(place_u, upper, lo, 1024), slots(place_l, lower, lo, 1024)], axis=1
            )
            pair_out[k - 1, :, :, lo : lo + 1024] = both.astype(jnp.bfloat16)

    def plane_refs(chunk):
        if chunk in (0, 4):
            return half_out.at[chunk // 4], half_in.at[chunk // 4]
        return pair_out.at[chunk - 1], pair_in.at[chunk - 1]

    def plane_copy(chunk, o):
        outgoing, incoming = plane_refs(chunk)
        target = (spot + o) % PLANE
        return pltpu.make_async_remote_copy(
            src_ref=outgoing.at[target],
            dst_ref=incoming.at[spot],
            send_sem=p_send.at[chunk * PLANE + target],
            recv_sem=p_recv.at[chunk * PLANE + spot],
            device_id=dev(z, target),
            device_id_type=MESH,
        )

    def plane_own(chunk):
        outgoing, incoming = plane_refs(chunk)
        return pltpu.make_async_copy(
            outgoing.at[spot], incoming.at[spot], p_recv.at[chunk * PLANE + spot]
        )

    def plane_start(chunk):
        for o in range(1, PLANE):
            plane_copy(chunk, o).start()
        plane_own(chunk).start()

    def plane_wait(chunk):
        outgoing, incoming = plane_refs(chunk)
        for o in range(1, PLANE):
            source = (spot + o) % PLANE
            pltpu.make_async_remote_copy(
                src_ref=outgoing.at[source],
                dst_ref=incoming.at[source],
                send_sem=p_send.at[chunk * PLANE + source],
                recv_sem=p_recv.at[chunk * PLANE + source],
                device_id=dev(z, source),
                device_id_type=MESH,
            ).wait_recv()
        plane_own(chunk).wait()

    def gated(gate_val, up_val):
        return gate_val / (1.0 + jnp.exp(-gate_val)) * up_val

    def give_back(values, dz_index):
        both = jnp.concatenate([values[:, :, : FFW // 2], values[:, :, FFW // 2 :]], axis=1)
        ret_out[dz_index] = both.astype(jnp.bfloat16)

    def ret_copy(dz, r):
        idx = (dz + NZ) % NZ
        return pltpu.make_async_remote_copy(
            src_ref=ret_out.at[idx, r],
            dst_ref=ret_in.at[ep],
            send_sem=r_send.at[idx * PLANE + r],
            recv_sem=r_recv.at[ep],
            device_id=dev(at_z(dz), r),
            device_id_type=MESH,
        )

    def ret_own():
        return pltpu.make_async_copy(ret_out.at[0, spot], ret_in.at[ep], r_recv.at[ep])

    def ret_start(dz):
        for o in range(PLANE):
            if dz == 0 and o == 0:
                ret_own().start()
            else:
                ret_copy(dz, (spot + o) % PLANE).start()

    def expert_half(chunk):
        plane_wait(chunk)
        for lo in range(0, FFW, 256):
            rows = half_in[chunk // 4].reshape(PLANE * 16, HALF)

            def halves(mat):
                first = jnp.dot(
                    rows, mat[:HALF, lo : lo + 256], preferred_element_type=jnp.float32
                ).reshape(PLANE, 16, 256)
                second = jnp.dot(
                    rows, mat[HALF:, lo : lo + 256], preferred_element_type=jnp.float32
                ).reshape(PLANE, 16, 256)
                return first[:, :CAP] + second[:, CAP:]

            act[:, :CAP, lo : lo + 256] = gated(halves(gate_w), halves(up_w))
        give_back(act[:, :CAP], chunk)
        ret_start(chunk)

    def expert_pair(k):
        plane_wait(k)
        for lo in range(0, FFW, 256):
            rows = pair_in[k - 1].reshape(PLANE * 16, D)
            gate_val = jnp.dot(rows, gate_w[:, lo : lo + 256], preferred_element_type=jnp.float32)
            up_val = jnp.dot(rows, up_w[:, lo : lo + 256], preferred_element_type=jnp.float32)
            act[:, :, lo : lo + 256] = gated(gate_val, up_val).reshape(PLANE, 16, 256)
        give_back(act[:, :CAP], k)
        give_back(act[:, CAP:], NZ - k)
        ret_start(k)
        ret_start(-k)

    hop(1, 1).start()
    hop(-1, 1).start()
    compact_half(0, z)
    plane_start(0)
    for k in (1, 2, 3):
        for sign in (1, -1):
            arrived(sign, k)
            hop(sign, k + 1).start()
        compact_pair(k)
        plane_start(k)
        if k == 1:
            for copy in w_copies:
                copy.wait()
            expert_half(0)
        if k == 3:
            expert_pair(1)
    arrived(1, 4)
    arrived(-1, 4)
    compact_half(1, at_z(4))
    plane_start(4)
    expert_pair(2)
    expert_pair(3)
    expert_half(4)

    for sign in (1, -1):
        for k in (1, 2, 3, 4):
            hop(sign, k).wait_send()
    for chunk in range(5):
        for o in range(1, PLANE):
            plane_copy(chunk, o).wait_send()

    def ret_sent(i, carry):
        dz_index = i // PLANE
        pltpu.make_async_remote_copy(
            src_ref=ret_out.at[dz_index, i % PLANE],
            dst_ref=ret_in.at[ep],
            send_sem=r_send.at[i],
            recv_sem=r_recv.at[ep],
            device_id=dev(at_z(dz_index), i % PLANE),
            device_id_type=MESH,
        ).wait_send()
        return carry

    for o in range(1, PLANE):
        ret_copy(0, (spot + o) % PLANE).wait_send()
    lax.fori_loop(PLANE, NZ * PLANE, ret_sent, 0)

    def ret_got(o, carry):
        expert = (ep + o) % (NZ * PLANE)
        pltpu.make_async_remote_copy(
            src_ref=ret_in.at[expert],
            dst_ref=ret_in.at[expert],
            send_sem=r_send.at[o],
            recv_sem=r_recv.at[expert],
            device_id={"ep": expert},
            device_id_type=MESH,
        ).wait_recv()
        return carry

    ret_own().wait()
    lax.fori_loop(1, NZ * PLANE, ret_got, 0)

    back = ret_in[...].reshape(NZ * PLANE * 16, FFW // 2)
    column = lax.broadcasted_iota(jnp.int32, (TOK * 8, NZ * PLANE * 16), 1)
    for half in (0, 1):
        pick = (column == pos_ref[...] + CAP * half).astype(jnp.float32).astype(jnp.bfloat16)
        got = jnp.dot(pick, back, preferred_element_type=jnp.float32)
        out_ref[:, half * (FFW // 2) : (half + 1) * (FFW // 2)] = (
            share_ref[...] * got
        ).astype(jnp.bfloat16)


def layer_call(rows, gate_weight, up_weight, pos, share):
    bf = jnp.bfloat16
    dma = pltpu.SemaphoreType.DMA
    vmem = pl.BlockSpec(memory_space=pltpu.VMEM)
    hbm = pl.BlockSpec(memory_space=pl.ANY)
    return pl.pallas_call(
        layer_kernel,
        out_shape=jax.ShapeDtypeStruct((TOK * 8, FFW), bf),
        in_specs=[vmem, hbm, hbm, vmem, vmem],
        out_specs=vmem,
        scratch_shapes=[
            pltpu.VMEM((NZ, TOK, D + META), bf),
            pltpu.VMEM((2, PLANE, 16, HALF), bf),
            pltpu.VMEM((3, PLANE, 16, D), bf),
            pltpu.VMEM((2, PLANE, 16, HALF), bf),
            pltpu.VMEM((3, PLANE, 16, D), bf),
            pltpu.VMEM((D, FFW), bf),
            pltpu.VMEM((D, FFW), bf),
            pltpu.VMEM((PLANE, 16, FFW), jnp.float32),
            pltpu.VMEM((NZ, PLANE, 16, FFW // 2), bf),
            pltpu.VMEM((NZ * PLANE, 16, FFW // 2), bf),
            dma((2,)),
            dma((8,)),
            dma((8,)),
            dma((5 * PLANE,)),
            dma((5 * PLANE,)),
            dma((NZ * PLANE,)),
            dma((NZ * PLANE,)),
        ],
        compiler_params=pltpu.CompilerParams(
            collective_id=0, has_side_effects=True, vmem_limit_bytes=48 * 1024 * 1024
        ),
        cost_estimate=pl.CostEstimate(
            flops=2 * 512 * D * 2 * FFW, bytes_accessed=2 * D * FFW * 2, transcendentals=512 * FFW
        ),
    )(rows, gate_weight, up_weight, pos, share)


def local(
    tokens,
    norm_gain,
    gate_weight,
    up_weight,
    route_ids,
    route_scores,
    queries,
    key_cache,
    value_cache,
    new_keys,
    new_values,
    cache_lengths,
):
    attended = attend_rows(queries, key_cache, value_cache, new_keys, new_values, cache_lengths)
    hidden = (tokens.astype(jnp.float32) + attended.astype(jnp.float32)).astype(jnp.bfloat16)
    normed = rms_rows(hidden, norm_gain)
    experts = lax.axis_size("ep")
    expert_ids = jnp.arange(experts, dtype=jnp.int32)
    route_hot = route_ids[:, :, None] == expert_ids[None, None, :]
    hit_mask = jnp.any(route_hot, axis=1).astype(jnp.int32)
    slot_rank = jnp.cumsum(hit_mask, axis=0) - hit_mask
    row_slot = jnp.sum(jnp.where(route_hot, slot_rank[:, None, :], 0), axis=2)
    meta = jnp.where(hit_mask == 1, slot_rank, -1).astype(jnp.bfloat16)
    meta = jnp.pad(meta, ((0, 0), (0, META - experts)), constant_values=-1)
    rows = jnp.concatenate([normed, meta], axis=1)
    route_share = route_scores / jnp.sum(route_scores, axis=1, keepdims=True)
    pos = (route_ids * 16 + row_slot).reshape(-1, 1)
    expert_terms = layer_call(rows, gate_weight, up_weight, pos, route_share.reshape(-1, 1))
    return (expert_terms.reshape(route_ids.shape[0], route_ids.shape[1], FFW), attended)


def solution(mesh):
    return jax.shard_map(
        local,
        mesh=mesh,
        in_specs=(
            P(("rep", "ep"), None),
            P(),
            P(("rep", "ep"), None, None),
            P(("rep", "ep"), None, None),
            P(("rep", "ep"), None),
            P(("rep", "ep"), None),
            P(("rep", "ep"), None),
            P(("rep", "ep"), None, None),
            P(("rep", "ep"), None, None),
            P(("rep", "ep"), None),
            P(("rep", "ep"), None),
            P(("rep", "ep")),
        ),
        out_specs=(P(("rep", "ep"), None, None), P(("rep", "ep"), None)),
        check_vma=False,
    )
```

```python
import jax
import jax.experimental.pallas as pl
import jax.experimental.pallas.tpu as pltpu
import jax.numpy as jnp
from jax import lax
from jax.sharding import PartitionSpec as P

HD = 128
D = 4096
FFW = 768
TOK = 32
CAP = 8
NZ = 8
PLANE = 8
META = 128
HALF = D // 2
MESH = pl.DeviceIdType.MESH


def attend_rows(
    queries_ref, keys_ref, values_ref, new_keys_ref, new_values_ref, lengths_ref, attended_ref
):
    rows, heads = 16, 16
    size = rows * heads
    row = lax.broadcasted_iota(jnp.int32, (size, size), 0) % rows
    lane = lax.broadcasted_iota(jnp.int32, (size, size), 1)
    own_row = lax.broadcasted_iota(jnp.int32, (size, rows), 0) % rows
    own_lane = lax.broadcasted_iota(jnp.int32, (size, rows), 1)
    factor = HD ** (-0.5)
    contract = (((1,), (1,)), ((), ()))
    for first in range(0, TOK, rows):
        part = slice(first, first + rows)
        repeat = (
            lax.broadcasted_iota(jnp.int32, (TOK, size), 0)
            == first + lax.broadcasted_iota(jnp.int32, (TOK, size), 1) // rows
        ).astype(jnp.float32)
        counts = jnp.broadcast_to(lengths_ref[...].astype(jnp.float32), (8, TOK))
        lengths = jnp.dot(counts, repeat, preferred_element_type=jnp.float32)[:1]
        live = (row == lane // rows) & ((lane % rows).astype(jnp.float32) < lengths)
        for kv in range(2):
            cols = slice(kv * HD, (kv + 1) * HD)
            query = jnp.concatenate(
                [
                    queries_ref[part, (kv * heads + g) * HD : (kv * heads + g + 1) * HD]
                    for g in range(heads)
                ],
                axis=0,
            )
            key = keys_ref[part, :, cols].reshape(size, HD)
            value = values_ref[part, :, cols].reshape(size, HD)
            scores = factor * lax.dot_general(
                query, key, contract, preferred_element_type=jnp.float32
            )
            scores = jnp.where(live, scores, -1e30)
            own = factor * lax.dot_general(
                query, new_keys_ref[part, cols], contract, preferred_element_type=jnp.float32
            )
            own = jnp.sum(jnp.where(own_row == own_lane, own, 0.0), axis=1, keepdims=True)
            top = jnp.maximum(jnp.max(scores, axis=1, keepdims=True), own)
            weights = jnp.where(live, jnp.exp(scores - top), 0.0)
            own_weight = jnp.exp(own - top)
            mass = jnp.sum(weights, axis=1, keepdims=True) + own_weight
            probs = (weights / mass).astype(jnp.bfloat16)
            own_prob = (own_weight / mass).astype(jnp.bfloat16).astype(jnp.float32)
            fresh = jnp.concatenate(
                [new_values_ref[part, cols].astype(jnp.float32)] * heads, axis=0
            )
            summed = jnp.dot(probs, value, preferred_element_type=jnp.float32) + own_prob * fresh
            for g in range(heads):
                attended_ref[part, (kv * heads + g) * HD : (kv * heads + g + 1) * HD] = summed[
                    g * rows : (g + 1) * rows
                ].astype(jnp.bfloat16)


def norm_rows(tokens_ref, attended_ref, gain_ref, rows_ref):
    step = 1024
    total = jnp.zeros((TOK, 1), jnp.float32)
    for lo in range(0, D, step):
        cols = slice(lo, lo + step)
        hidden = tokens_ref[:, cols].astype(jnp.float32) + attended_ref[:, cols].astype(
            jnp.float32
        )
        hidden = hidden.astype(jnp.bfloat16)
        rows_ref[:, cols] = hidden
        hidden = hidden.astype(jnp.float32)
        total = total + jnp.sum(hidden * hidden, axis=1, keepdims=True)
    scale = lax.rsqrt(total / D + 1e-06)
    for lo in range(0, D, step):
        cols = slice(lo, lo + step)
        hidden = rows_ref[:, cols].astype(jnp.float32)
        rows_ref[:, cols] = (hidden * scale * gain_ref[:, cols]).astype(jnp.bfloat16)


def slot_ranks(ids_ref):
    expert = lax.broadcasted_iota(jnp.int32, (META, TOK), 0)
    hit = jnp.zeros((META, TOK), jnp.float32)
    for k in range(8):
        hit = hit + (expert == ids_ref[k : k + 1, :]).astype(jnp.float32)
    row = lax.broadcasted_iota(jnp.int32, (TOK, TOK), 0)
    col = lax.broadcasted_iota(jnp.int32, (TOK, TOK), 1)
    hit = hit.astype(jnp.bfloat16)

    def over_rows(mat):
        return lax.dot_general(
            mat.astype(jnp.float32).astype(jnp.bfloat16),
            hit,
            (((1,), (1,)), ((), ())),
            preferred_element_type=jnp.float32,
        )

    by_expert = jnp.dot(
        hit,
        (row < col).astype(jnp.float32).astype(jnp.bfloat16),
        preferred_element_type=jnp.float32,
    )
    meta = jnp.where(over_rows(row == col) > 0.0, over_rows(row > col), -1.0)
    return meta.astype(jnp.bfloat16), by_expert


def pick_columns(ids_ref, scores_ref, rank, pos_col, share_col):
    expert = lax.broadcasted_iota(jnp.int32, (META, TOK), 0)
    slot = jnp.concatenate(
        [
            jnp.sum(jnp.where(expert == ids_ref[k : k + 1, :], rank, 0.0), axis=0, keepdims=True)
            for k in range(8)
        ],
        axis=0,
    )
    score = scores_ref[...]
    share = score / jnp.sum(score, axis=0, keepdims=True)
    spread = (
        lax.broadcasted_iota(jnp.int32, (TOK * 8, TOK), 0) // 8
        == lax.broadcasted_iota(jnp.int32, (TOK * 8, TOK), 1)
    ).astype(jnp.float32)
    mine = lax.broadcasted_iota(jnp.int32, (TOK * 8, 8), 0) % 8 == lax.broadcasted_iota(
        jnp.int32, (TOK * 8, 8), 1
    )

    def column(values):
        every = lax.dot_general(
            spread,
            values,
            (((1,), (1,)), ((), ())),
            precision=lax.Precision.HIGHEST,
            preferred_element_type=jnp.float32,
        )
        return jnp.sum(jnp.where(mine, every, 0.0), axis=1, keepdims=True)

    pos_col[...] = column(ids_ref[...].astype(jnp.float32) * 16.0 + slot).astype(jnp.int32)
    share_col[...] = column(share)


def layer_kernel(
    tokens_hbm, gain_hbm, gate_hbm, up_hbm, ids_hbm, scores_hbm, queries_hbm, keys_hbm,
    values_hbm, new_keys_hbm, new_values_hbm, lengths_hbm, out_ref, attended_ref,
    tokens_ref, gain_ref, ids_ref, scores_ref, queries_ref, keys_ref,
    values_ref, new_keys_ref, new_values_ref, lengths_ref,
    raw, side, half_out, low_out, high_out, half_in, low_in, high_in,
    gate_w, up_w, act, ret_out, ret_in, pos_col, share_col,
    in_sem, w_sem, z_send, z_recv, n_send, n_recv, p_send, p_recv, h_send, h_recv, r_send, r_recv,
):
    ep = lax.axis_index("ep")
    z = ep // PLANE
    spot = ep % PLANE
    x = spot // 2
    core = spot % 2
    turn = 1 - 2 * core

    def at_x(steps):
        return (x + steps * turn + 4) % 4

    def spot_of(steps, other):
        return at_x(steps) * 2 + (core + other) % 2

    def at_z(dz):
        return (z + dz + NZ) % NZ

    def dev(zz, ss):
        return {"ep": zz * PLANE + ss}

    in_copies = [
        pltpu.make_async_copy(source, target, in_sem.at[i])
        for i, (source, target) in enumerate(
            (
                (queries_hbm, queries_ref),
                (keys_hbm, keys_ref),
                (values_hbm, values_ref),
                (new_keys_hbm, new_keys_ref),
                (new_values_hbm, new_values_ref),
                (lengths_hbm, lengths_ref),
                (tokens_hbm, tokens_ref),
                (gain_hbm, gain_ref),
                (ids_hbm, ids_ref),
                (scores_hbm, scores_ref),
            )
        )
    ]
    w_copies = [
        pltpu.make_async_copy(gate_hbm.at[0], gate_w, w_sem.at[0]),
        pltpu.make_async_copy(up_hbm.at[0], up_w, w_sem.at[1]),
    ]
    for copy in in_copies + w_copies:
        copy.start()
    barrier = pltpu.get_barrier_semaphore()

    def greet(o, carry):
        pl.semaphore_signal(
            barrier, inc=1, device_id={"ep": (ep + o) % (NZ * PLANE)}, device_id_type=MESH
        )
        return carry

    lax.fori_loop(1, NZ * PLANE, greet, 0)
    for copy in in_copies:
        copy.wait()
    attend_rows(
        queries_ref, keys_ref, values_ref, new_keys_ref, new_values_ref, lengths_ref, attended_ref
    )
    norm_rows(tokens_ref, attended_ref, gain_ref, raw.at[z])
    meta, rank = slot_ranks(ids_ref)
    raw[z, :, D:] = meta
    pl.semaphore_wait(barrier, NZ * PLANE - 1)

    def hop(sign, k):
        block = raw.at[at_z(-sign * (k - 1))]
        if k == 4:
            block = block.at[pl.ds(0 if sign > 0 else 16, 16)]
        idx = (k - 1) + (0 if sign > 0 else 4)
        return pltpu.make_async_remote_copy(
            src_ref=block,
            dst_ref=block,
            send_sem=z_send.at[idx],
            recv_sem=z_recv.at[idx],
            device_id=dev(at_z(sign), spot),
            device_id_type=MESH,
        )

    def arrived(sign, k):
        block = raw.at[at_z(-sign * k)]
        if k == 4:
            block = block.at[pl.ds(0 if sign > 0 else 16, 16)]
        idx = (k - 1) + (0 if sign > 0 else 4)
        pltpu.make_async_remote_copy(
            src_ref=block,
            dst_ref=block,
            send_sem=z_send.at[idx],
            recv_sem=z_recv.at[idx],
            device_id=dev(at_z(sign), spot),
            device_id_type=MESH,
        ).wait_recv()

    def side_copy(idx, block_out, block_in, device):
        return pltpu.make_async_remote_copy(
            src_ref=block_out,
            dst_ref=block_in,
            send_sem=n_send.at[idx],
            recv_sem=n_recv.at[idx],
            device_id=device,
            device_id_type=MESH,
        )

    def side_first():
        return side_copy(
            0, raw.at[z, :, pl.ds(HALF, HALF + META)], side.at[z], dev(z, spot_of(1, 0))
        )

    def side_hop(sign, k):
        block = side.at[at_z(-sign * (k - 1))]
        return side_copy(k if sign > 0 else k + 3, block, block, dev(at_z(sign), spot))

    def side_arrived(sign, k):
        block = side.at[at_z(-sign * k)]
        side_copy(k if sign > 0 else k + 3, block, block, dev(at_z(sign), spot)).wait_recv()

    def expert_hot(near, far):
        slot_row = lax.broadcasted_iota(jnp.int32, (4 * CAP, META), 0) // CAP
        lane = lax.broadcasted_iota(jnp.int32, (4 * CAP, META), 1)
        spots = jnp.where(slot_row < 2, near * 2 + slot_row, far * 2 + slot_row - 2)
        return (lane == z * PLANE + spots).astype(jnp.bfloat16)

    slot_row = lax.broadcasted_iota(jnp.int32, (PLANE * CAP, META), 0)
    lane = lax.broadcasted_iota(jnp.int32, (PLANE * CAP, META), 1)
    plane_hot = (lane == z * PLANE + slot_row // CAP).astype(jnp.bfloat16)
    own_hot = expert_hot(x, at_x(-1))
    side_hot = expert_hot(x, at_x(1))

    def placing(hot, meta):
        ranks = lax.dot_general(
            hot, meta, (((1,), (1,)), ((), ())), preferred_element_type=jnp.float32
        )
        wanted = lax.broadcasted_iota(jnp.int32, ranks.shape, 0) % CAP
        return (ranks == wanted.astype(jnp.float32)).astype(jnp.float32).astype(jnp.bfloat16)

    def slots(place, block):
        got = jnp.dot(place, block, preferred_element_type=jnp.float32)
        return got.reshape(place.shape[0] // CAP, CAP, block.shape[1])

    def compact_half(i, zz):
        place = placing(plane_hot, raw[zz, :, D:])
        for lo in range(0, HALF, 1024):
            both = jnp.concatenate(
                [
                    slots(place, raw[zz, :, lo : lo + 1024]),
                    slots(place, raw[zz, :, HALF + lo : HALF + lo + 1024]),
                ],
                axis=1,
            )
            half_out[i, :, :, lo : lo + 1024] = both.astype(jnp.bfloat16)

    def compact_pair(k, hot, source, meta_at, first, out, place_at):
        upper, lower = at_z(k), at_z(-k)
        place_u = placing(hot, source[upper, :, meta_at : meta_at + META])
        place_l = placing(hot, source[lower, :, meta_at : meta_at + META])
        for lo in range(0, HALF, 1024):
            both = jnp.concatenate(
                [
                    slots(place_u, source[upper, :, first + lo : first + lo + 1024]),
                    slots(place_l, source[lower, :, first + lo : first + lo + 1024]),
                ],
                axis=1,
            )
            rows = hot.shape[0] // CAP
            out[k - 1, place_at : place_at + rows, :, lo : lo + 1024] = both.astype(jnp.bfloat16)

    def plane_refs(chunk):
        if chunk in (0, 4):
            return half_out.at[chunk // 4], half_in.at[chunk // 4]
        return low_out.at[chunk - 1], low_in.at[chunk - 1]

    def plane_copy(chunk, o):
        outgoing, incoming = plane_refs(chunk)
        target = (spot + o) % PLANE
        return pltpu.make_async_remote_copy(
            src_ref=outgoing.at[target],
            dst_ref=incoming.at[spot],
            send_sem=p_send.at[chunk * PLANE + target],
            recv_sem=p_recv.at[chunk * PLANE + spot],
            device_id=dev(z, target),
            device_id_type=MESH,
        )

    def plane_own(chunk):
        outgoing, incoming = plane_refs(chunk)
        return pltpu.make_async_copy(
            outgoing.at[spot], incoming.at[spot], p_recv.at[chunk * PLANE + spot]
        )

    def plane_start(chunk):
        for o in range(1, PLANE):
            plane_copy(chunk, o).start()
        plane_own(chunk).start()

    def plane_wait(chunk):
        outgoing, incoming = plane_refs(chunk)
        for o in range(1, PLANE):
            source = (spot + o) % PLANE
            pltpu.make_async_remote_copy(
                src_ref=outgoing.at[source],
                dst_ref=incoming.at[source],
                send_sem=p_send.at[chunk * PLANE + source],
                recv_sem=p_recv.at[chunk * PLANE + source],
                device_id=dev(z, source),
                device_id_type=MESH,
            ).wait_recv()
        plane_own(chunk).wait()

    def high_copy(k, place, steps, other, origin):
        return pltpu.make_async_remote_copy(
            src_ref=high_out.at[k - 1, place],
            dst_ref=high_in.at[k - 1, origin],
            send_sem=h_send.at[(k - 1) * PLANE + place],
            recv_sem=h_recv.at[(k - 1) * PLANE + origin],
            device_id=dev(z, spot_of(steps, other)),
            device_id_type=MESH,
        )

    def high_local(k, place, origin):
        return pltpu.make_async_copy(
            high_out.at[k - 1, place],
            high_in.at[k - 1, origin],
            h_recv.at[(k - 1) * PLANE + origin],
        )

    def high_list(k, base, far, origin):
        return [
            high_copy(k, base + (core + 1) % 2, 0, 1, origin),
            high_copy(k, base + 2 + core, far, 0, origin),
            high_copy(k, base + 2 + (core + 1) % 2, far, 1, origin),
        ]

    def high_own(k):
        return high_list(k, 0, -1, spot)

    def high_side(k):
        return high_list(k, 4, 1, spot_of(-1, 0))

    def high_start(k, base, copies, origin):
        for copy in copies:
            copy.start()
        high_local(k, base + core, origin).start()

    def high_wait(k):
        for steps, other in ((1, 0), (2, 0), (0, 1), (1, 1), (2, 1), (3, 1)):
            high_copy(k, 0, 0, 1, spot_of(steps, other)).wait_recv()
        high_local(k, core, spot).wait()
        high_local(k, 4 + core, spot_of(-1, 0)).wait()

    def gated(gate_val, up_val):
        return gate_val / (1.0 + jnp.exp(-gate_val)) * up_val

    def give_back(values, dz_index):
        both = jnp.concatenate([values[:, :, : FFW // 2], values[:, :, FFW // 2 :]], axis=1)
        ret_out[dz_index] = both.astype(jnp.bfloat16)

    def ret_copy(dz, r):
        idx = (dz + NZ) % NZ
        return pltpu.make_async_remote_copy(
            src_ref=ret_out.at[idx, r],
            dst_ref=ret_in.at[ep],
            send_sem=r_send.at[idx * PLANE + r],
            recv_sem=r_recv.at[ep],
            device_id=dev(at_z(dz), r),
            device_id_type=MESH,
        )

    def ret_own():
        return pltpu.make_async_copy(ret_out.at[0, spot], ret_in.at[ep], r_recv.at[ep])

    def ret_start(dz):
        for o in range(PLANE):
            if dz == 0 and o == 0:
                ret_own().start()
            else:
                ret_copy(dz, (spot + o) % PLANE).start()

    def expert_half(chunk):
        plane_wait(chunk)
        for lo in range(0, FFW, 256):
            rows = half_in[chunk // 4].reshape(PLANE * 16, HALF)

            def halves(mat):
                first = jnp.dot(
                    rows, mat[:HALF, lo : lo + 256], preferred_element_type=jnp.float32
                ).reshape(PLANE, 16, 256)
                second = jnp.dot(
                    rows, mat[HALF:, lo : lo + 256], preferred_element_type=jnp.float32
                ).reshape(PLANE, 16, 256)
                return first[:, :CAP] + second[:, CAP:]

            act[:, :CAP, lo : lo + 256] = gated(halves(gate_w), halves(up_w))
        give_back(act[:, :CAP], chunk)
        ret_start(chunk)

    def expert_pair(k):
        plane_wait(k)
        high_wait(k)
        for lo in range(0, FFW, 256):
            low = low_in[k - 1].reshape(PLANE * 16, HALF)
            high = high_in[k - 1].reshape(PLANE * 16, HALF)

            def both(mat):
                return jnp.dot(
                    low, mat[:HALF, lo : lo + 256], preferred_element_type=jnp.float32
                ) + jnp.dot(high, mat[HALF:, lo : lo + 256], preferred_element_type=jnp.float32)

            act[:, :, lo : lo + 256] = gated(both(gate_w), both(up_w)).reshape(PLANE, 16, 256)
        give_back(act[:, :CAP], k)
        give_back(act[:, CAP:], NZ - k)
        ret_start(k)
        ret_start(-k)

    hop(1, 1).start()
    hop(-1, 1).start()
    side_first().start()
    compact_half(0, z)
    plane_start(0)
    pick_columns(ids_ref, scores_ref, rank, pos_col, share_col)
    side_copy(0, side.at[z], side.at[z], dev(z, spot_of(1, 0))).wait_recv()
    side_hop(1, 1).start()
    side_hop(-1, 1).start()
    for k in (1, 2, 3):
        for sign in (1, -1):
            arrived(sign, k)
            hop(sign, k + 1).start()
        compact_pair(k, plane_hot, raw, D, 0, low_out, 0)
        plane_start(k)
        compact_pair(k, own_hot, raw, D, HALF, high_out, 0)
        high_start(k, 0, high_own(k), spot)
        for sign in (1, -1):
            side_arrived(sign, k)
            if k < 3:
                side_hop(sign, k + 1).start()
        compact_pair(k, side_hot, side, HALF, 0, high_out, 4)
        high_start(k, 4, high_side(k), spot_of(-1, 0))
        if k == 1:
            for copy in w_copies:
                copy.wait()
            expert_half(0)
        else:
            expert_pair(k - 1)
    arrived(1, 4)
    arrived(-1, 4)
    compact_half(1, at_z(4))
    plane_start(4)
    expert_pair(3)
    expert_half(4)

    side_first().wait_send()
    for sign in (1, -1):
        for k in (1, 2, 3, 4):
            hop(sign, k).wait_send()
        for k in (1, 2, 3):
            side_hop(sign, k).wait_send()
    for k in (1, 2, 3):
        for copy in high_own(k) + high_side(k):
            copy.wait_send()
    for chunk in range(5):
        for o in range(1, PLANE):
            plane_copy(chunk, o).wait_send()

    def ret_sent(i, carry):
        dz_index = i // PLANE
        pltpu.make_async_remote_copy(
            src_ref=ret_out.at[dz_index, i % PLANE],
            dst_ref=ret_in.at[ep],
            send_sem=r_send.at[i],
            recv_sem=r_recv.at[ep],
            device_id=dev(at_z(dz_index), i % PLANE),
            device_id_type=MESH,
        ).wait_send()
        return carry

    for o in range(1, PLANE):
        ret_copy(0, (spot + o) % PLANE).wait_send()
    lax.fori_loop(PLANE, NZ * PLANE, ret_sent, 0)

    def ret_got(o, carry):
        expert = (ep + o) % (NZ * PLANE)
        pltpu.make_async_remote_copy(
            src_ref=ret_in.at[expert],
            dst_ref=ret_in.at[expert],
            send_sem=r_send.at[o],
            recv_sem=r_recv.at[expert],
            device_id={"ep": expert},
            device_id_type=MESH,
        ).wait_recv()
        return carry

    ret_own().wait()
    lax.fori_loop(1, NZ * PLANE, ret_got, 0)

    back = ret_in[...].reshape(NZ * PLANE * 16, FFW // 2)
    column = lax.broadcasted_iota(jnp.int32, (TOK * 8, NZ * PLANE * 16), 1)
    for half in (0, 1):
        pick = (column == pos_col[...] + CAP * half).astype(jnp.float32).astype(jnp.bfloat16)
        got = jnp.dot(pick, back, preferred_element_type=jnp.float32)
        out_ref[:, half * (FFW // 2) : (half + 1) * (FFW // 2)] = (
            share_col[...] * got
        ).astype(jnp.bfloat16)


def layer_call(*args):
    bf = jnp.bfloat16
    dma = pltpu.SemaphoreType.DMA
    vmem = pl.BlockSpec(memory_space=pltpu.VMEM)
    hbm = pl.BlockSpec(memory_space=pl.ANY)
    return pl.pallas_call(
        layer_kernel,
        out_shape=(
            jax.ShapeDtypeStruct((TOK * 8, FFW), bf),
            jax.ShapeDtypeStruct((TOK, D), bf),
        ),
        in_specs=[hbm] * 12,
        out_specs=(vmem, vmem),
        scratch_shapes=[
            pltpu.VMEM((TOK, D), bf),
            pltpu.VMEM((1, D), jnp.float32),
            pltpu.VMEM((8, TOK), jnp.int32),
            pltpu.VMEM((8, TOK), jnp.float32),
            pltpu.VMEM((TOK, D), bf),
            pltpu.VMEM((TOK, 16, 2 * HD), bf),
            pltpu.VMEM((TOK, 16, 2 * HD), bf),
            pltpu.VMEM((TOK, 2 * HD), bf),
            pltpu.VMEM((TOK, 2 * HD), bf),
            pltpu.VMEM((1, TOK), jnp.int32),
            pltpu.VMEM((NZ, TOK, D + META), bf),
            pltpu.VMEM((NZ, TOK, HALF + META), bf),
            pltpu.VMEM((2, PLANE, 16, HALF), bf),
            pltpu.VMEM((3, PLANE, 16, HALF), bf),
            pltpu.VMEM((3, PLANE, 16, HALF), bf),
            pltpu.VMEM((2, PLANE, 16, HALF), bf),
            pltpu.VMEM((3, PLANE, 16, HALF), bf),
            pltpu.VMEM((3, PLANE, 16, HALF), bf),
            pltpu.VMEM((D, FFW), bf),
            pltpu.VMEM((D, FFW), bf),
            pltpu.VMEM((PLANE, 16, FFW), jnp.float32),
            pltpu.VMEM((NZ, PLANE, 16, FFW // 2), bf),
            pltpu.VMEM((NZ * PLANE, 16, FFW // 2), bf),
            pltpu.VMEM((TOK * 8, 1), jnp.int32),
            pltpu.VMEM((TOK * 8, 1), jnp.float32),
            dma((10,)),
            dma((2,)),
            dma((8,)),
            dma((8,)),
            dma((7,)),
            dma((7,)),
            dma((5 * PLANE,)),
            dma((5 * PLANE,)),
            dma((3 * PLANE,)),
            dma((3 * PLANE,)),
            dma((NZ * PLANE,)),
            dma((NZ * PLANE,)),
        ],
        compiler_params=pltpu.CompilerParams(
            collective_id=0, has_side_effects=True, vmem_limit_bytes=60 * 1024 * 1024
        ),
        cost_estimate=pl.CostEstimate(
            flops=2 * 512 * D * 2 * FFW, bytes_accessed=2 * D * FFW * 2, transcendentals=512 * FFW
        ),
    )(*args)


def hand_over_kernel(terms_in, attended_in, terms_out, attended_out, terms_buf, attended_buf, sem):
    arriving, leaving = [], []
    for source, middle, target in (
        (terms_in, terms_buf, terms_out),
        (attended_in, attended_buf, attended_out),
    ):
        step = source.shape[0] // 2
        for part in range(2):
            rows = pl.ds(part * step, step)
            i = 2 * len(arriving)
            arriving.append(pltpu.make_async_copy(source.at[rows], middle.at[rows], sem.at[i]))
            leaving.append(pltpu.make_async_copy(middle.at[rows], target.at[rows], sem.at[i + 1]))
    for copy in arriving:
        copy.start()
    for first, second in zip(arriving, leaving):
        first.wait()
        second.start()
    for copy in leaving:
        copy.wait()


def hand_over(terms, attended):
    hbm = pl.BlockSpec(memory_space=pl.ANY)
    return pl.pallas_call(
        hand_over_kernel,
        out_shape=(
            jax.ShapeDtypeStruct(terms.shape, terms.dtype),
            jax.ShapeDtypeStruct(attended.shape, attended.dtype),
        ),
        in_specs=[hbm, hbm],
        out_specs=(hbm, hbm),
        scratch_shapes=[
            pltpu.VMEM(terms.shape, terms.dtype),
            pltpu.VMEM(attended.shape, attended.dtype),
            pltpu.SemaphoreType.DMA((8,)),
        ],
        compiler_params=pltpu.CompilerParams(vmem_limit_bytes=60 * 1024 * 1024),
    )(terms, attended)


def local(
    tokens,
    norm_gain,
    gate_weight,
    up_weight,
    route_ids,
    route_scores,
    queries,
    key_cache,
    value_cache,
    new_keys,
    new_values,
    cache_lengths,
):
    expert_terms, attended = layer_call(
        tokens,
        norm_gain.reshape(1, -1),
        gate_weight,
        up_weight,
        route_ids.T,
        route_scores.T,
        queries,
        key_cache,
        value_cache,
        new_keys,
        new_values,
        cache_lengths.reshape(1, -1),
    )
    expert_terms, attended = hand_over(expert_terms, attended)
    return (expert_terms.reshape(route_ids.shape[0], route_ids.shape[1], FFW), attended)


def solution(mesh):
    return jax.shard_map(
        local,
        mesh=mesh,
        in_specs=(
            P(("rep", "ep"), None),
            P(),
            P(("rep", "ep"), None, None),
            P(("rep", "ep"), None, None),
            P(("rep", "ep"), None),
            P(("rep", "ep"), None),
            P(("rep", "ep"), None),
            P(("rep", "ep"), None, None),
            P(("rep", "ep"), None, None),
            P(("rep", "ep"), None),
            P(("rep", "ep"), None),
            P(("rep", "ep")),
        ),
        out_specs=(P(("rep", "ep"), None, None), P(("rep", "ep"), None)),
        check_vma=False,
    )
```

```python
import jax
import jax.experimental.pallas as pl
import jax.experimental.pallas.tpu as pltpu
import jax.numpy as jnp
from jax import lax
from jax.sharding import PartitionSpec as P

HD = 128
D = 4096
FFW = 768
TOK = 32
CAP = 8
NZ = 8
PLANE = 8
META = 128
HALF = D // 2
MESH = pl.DeviceIdType.MESH


def attend_rows(
    queries_ref, keys_ref, values_ref, new_keys_ref, new_values_ref, lengths_ref, attended_ref
):
    rows, heads = 16, 16
    size = rows * heads
    row = lax.broadcasted_iota(jnp.int32, (size, size), 0) % rows
    lane = lax.broadcasted_iota(jnp.int32, (size, size), 1)
    own_row = lax.broadcasted_iota(jnp.int32, (size, rows), 0) % rows
    own_lane = lax.broadcasted_iota(jnp.int32, (size, rows), 1)
    factor = HD ** (-0.5)
    contract = (((1,), (1,)), ((), ()))
    for first in range(0, TOK, rows):
        part = slice(first, first + rows)
        repeat = (
            lax.broadcasted_iota(jnp.int32, (TOK, size), 0)
            == first + lax.broadcasted_iota(jnp.int32, (TOK, size), 1) // rows
        ).astype(jnp.float32)
        counts = jnp.broadcast_to(lengths_ref[...].astype(jnp.float32), (8, TOK))
        lengths = jnp.dot(counts, repeat, preferred_element_type=jnp.float32)[:1]
        live = (row == lane // rows) & ((lane % rows).astype(jnp.float32) < lengths)
        for kv in range(2):
            cols = slice(kv * HD, (kv + 1) * HD)
            query = jnp.concatenate(
                [
                    queries_ref[part, (kv * heads + g) * HD : (kv * heads + g + 1) * HD]
                    for g in range(heads)
                ],
                axis=0,
            )
            key = keys_ref[part, :, cols].reshape(size, HD)
            value = values_ref[part, :, cols].reshape(size, HD)
            scores = factor * lax.dot_general(
                query, key, contract, preferred_element_type=jnp.float32
            )
            scores = jnp.where(live, scores, -1e30)
            own = factor * lax.dot_general(
                query, new_keys_ref[part, cols], contract, preferred_element_type=jnp.float32
            )
            own = jnp.sum(jnp.where(own_row == own_lane, own, 0.0), axis=1, keepdims=True)
            top = jnp.maximum(jnp.max(scores, axis=1, keepdims=True), own)
            weights = jnp.where(live, jnp.exp(scores - top), 0.0)
            own_weight = jnp.exp(own - top)
            mass = jnp.sum(weights, axis=1, keepdims=True) + own_weight
            probs = (weights / mass).astype(jnp.bfloat16)
            own_prob = (own_weight / mass).astype(jnp.bfloat16).astype(jnp.float32)
            fresh = jnp.concatenate(
                [new_values_ref[part, cols].astype(jnp.float32)] * heads, axis=0
            )
            summed = jnp.dot(probs, value, preferred_element_type=jnp.float32) + own_prob * fresh
            for g in range(heads):
                attended_ref[part, (kv * heads + g) * HD : (kv * heads + g + 1) * HD] = summed[
                    g * rows : (g + 1) * rows
                ].astype(jnp.bfloat16)


def norm_rows(tokens_ref, attended_ref, gain_ref, rows_ref):
    step = 1024
    total = jnp.zeros((TOK, 1), jnp.float32)
    for lo in range(0, D, step):
        cols = slice(lo, lo + step)
        hidden = tokens_ref[:, cols].astype(jnp.float32) + attended_ref[:, cols].astype(
            jnp.float32
        )
        hidden = hidden.astype(jnp.bfloat16)
        rows_ref[:, cols] = hidden
        hidden = hidden.astype(jnp.float32)
        total = total + jnp.sum(hidden * hidden, axis=1, keepdims=True)
    scale = lax.rsqrt(total / D + 1e-06)
    for lo in range(0, D, step):
        cols = slice(lo, lo + step)
        hidden = rows_ref[:, cols].astype(jnp.float32)
        rows_ref[:, cols] = (hidden * scale * gain_ref[:, cols]).astype(jnp.bfloat16)


def slot_ranks(ids_ref):
    expert = lax.broadcasted_iota(jnp.int32, (META, TOK), 0)
    hit = jnp.zeros((META, TOK), jnp.float32)
    for k in range(8):
        hit = hit + (expert == ids_ref[k : k + 1, :]).astype(jnp.float32)
    row = lax.broadcasted_iota(jnp.int32, (TOK, TOK), 0)
    col = lax.broadcasted_iota(jnp.int32, (TOK, TOK), 1)
    hit = hit.astype(jnp.bfloat16)

    def over_rows(mat):
        return lax.dot_general(
            mat.astype(jnp.float32).astype(jnp.bfloat16),
            hit,
            (((1,), (1,)), ((), ())),
            preferred_element_type=jnp.float32,
        )

    by_expert = jnp.dot(
        hit,
        (row < col).astype(jnp.float32).astype(jnp.bfloat16),
        preferred_element_type=jnp.float32,
    )
    meta = jnp.where(over_rows(row == col) > 0.0, over_rows(row > col), -1.0)
    return meta.astype(jnp.bfloat16), by_expert


def pick_columns(ids_ref, scores_ref, rank, pos_col, share_col):
    expert = lax.broadcasted_iota(jnp.int32, (META, TOK), 0)
    slot = jnp.concatenate(
        [
            jnp.sum(jnp.where(expert == ids_ref[k : k + 1, :], rank, 0.0), axis=0, keepdims=True)
            for k in range(8)
        ],
        axis=0,
    )
    score = scores_ref[...]
    share = score / jnp.sum(score, axis=0, keepdims=True)
    spread = (
        lax.broadcasted_iota(jnp.int32, (TOK * 8, TOK), 0) // 8
        == lax.broadcasted_iota(jnp.int32, (TOK * 8, TOK), 1)
    ).astype(jnp.float32)
    mine = lax.broadcasted_iota(jnp.int32, (TOK * 8, 8), 0) % 8 == lax.broadcasted_iota(
        jnp.int32, (TOK * 8, 8), 1
    )

    def column(values):
        every = lax.dot_general(
            spread,
            values,
            (((1,), (1,)), ((), ())),
            precision=lax.Precision.HIGHEST,
            preferred_element_type=jnp.float32,
        )
        return jnp.sum(jnp.where(mine, every, 0.0), axis=1, keepdims=True)

    pos_col[...] = column(ids_ref[...].astype(jnp.float32) * 16.0 + slot).astype(jnp.int32)
    share_col[...] = column(share)


def layer_kernel(
    tokens_hbm, gain_hbm, gate_hbm, up_hbm, ids_hbm, scores_hbm, queries_hbm, keys_hbm,
    values_hbm, new_keys_hbm, new_values_hbm, lengths_hbm, out_ref, attended_ref,
    tokens_ref, gain_ref, ids_ref, scores_ref, queries_ref, keys_ref,
    values_ref, new_keys_ref, new_values_ref, lengths_ref,
    raw, side, half_out, low_out, high_out, half_in, low_in, high_in,
    gate_w, up_w, act, ret_out, ret_in, pos_col, share_col,
    in_sem, w_sem, z_send, z_recv, n_send, n_recv, p_send, p_recv, h_send, h_recv, r_send, r_recv,
):
    ep = lax.axis_index("ep")
    z = ep // PLANE
    spot = ep % PLANE
    x = spot // 2
    core = spot % 2
    turn = 1 - 2 * core

    def at_x(steps):
        return (x + steps * turn + 4) % 4

    def spot_of(steps, other):
        return at_x(steps) * 2 + (core + other) % 2

    def at_z(dz):
        return (z + dz + NZ) % NZ

    def dev(zz, ss):
        return {"ep": zz * PLANE + ss}

    in_copies = [
        pltpu.make_async_copy(source, target, in_sem.at[i])
        for i, (source, target) in enumerate(
            (
                (queries_hbm, queries_ref),
                (keys_hbm, keys_ref),
                (values_hbm, values_ref),
                (new_keys_hbm, new_keys_ref),
                (new_values_hbm, new_values_ref),
                (lengths_hbm, lengths_ref),
                (tokens_hbm, tokens_ref),
                (gain_hbm, gain_ref),
                (ids_hbm, ids_ref),
                (scores_hbm, scores_ref),
            )
        )
    ]
    w_copies = [
        pltpu.make_async_copy(gate_hbm.at[0], gate_w, w_sem.at[0]),
        pltpu.make_async_copy(up_hbm.at[0], up_w, w_sem.at[1]),
    ]
    for copy in in_copies + w_copies:
        copy.start()
    barrier = pltpu.get_barrier_semaphore()

    for sign in (1, -1):
        pl.semaphore_signal(barrier, inc=1, device_id=dev(at_z(sign), spot), device_id_type=MESH)
    for o in range(1, PLANE):
        pl.semaphore_signal(
            barrier, inc=1, device_id=dev(z, (spot + o) % PLANE), device_id_type=MESH
        )
    for copy in in_copies:
        copy.wait()
    attend_rows(
        queries_ref, keys_ref, values_ref, new_keys_ref, new_values_ref, lengths_ref, attended_ref
    )
    norm_rows(tokens_ref, attended_ref, gain_ref, raw.at[z])
    meta, rank = slot_ranks(ids_ref)
    raw[z, :, D:] = meta
    pl.semaphore_wait(barrier, PLANE + 1)

    def hop(sign, k):
        block = raw.at[at_z(-sign * (k - 1))]
        if k == 4:
            block = block.at[pl.ds(0 if sign > 0 else 16, 16)]
        idx = (k - 1) + (0 if sign > 0 else 4)
        return pltpu.make_async_remote_copy(
            src_ref=block,
            dst_ref=block,
            send_sem=z_send.at[idx],
            recv_sem=z_recv.at[idx],
            device_id=dev(at_z(sign), spot),
            device_id_type=MESH,
        )

    def arrived(sign, k):
        block = raw.at[at_z(-sign * k)]
        if k == 4:
            block = block.at[pl.ds(0 if sign > 0 else 16, 16)]
        idx = (k - 1) + (0 if sign > 0 else 4)
        pltpu.make_async_remote_copy(
            src_ref=block,
            dst_ref=block,
            send_sem=z_send.at[idx],
            recv_sem=z_recv.at[idx],
            device_id=dev(at_z(sign), spot),
            device_id_type=MESH,
        ).wait_recv()

    def side_copy(idx, block_out, block_in, device):
        return pltpu.make_async_remote_copy(
            src_ref=block_out,
            dst_ref=block_in,
            send_sem=n_send.at[idx],
            recv_sem=n_recv.at[idx],
            device_id=device,
            device_id_type=MESH,
        )

    def side_first():
        return side_copy(
            0, raw.at[z, :, pl.ds(HALF, HALF + META)], side.at[z], dev(z, spot_of(1, 0))
        )

    def side_hop(sign, k):
        block = side.at[at_z(-sign * (k - 1))]
        return side_copy(k if sign > 0 else k + 3, block, block, dev(at_z(sign), spot))

    def side_arrived(sign, k):
        block = side.at[at_z(-sign * k)]
        side_copy(k if sign > 0 else k + 3, block, block, dev(at_z(sign), spot)).wait_recv()

    def expert_hot(near, far):
        slot_row = lax.broadcasted_iota(jnp.int32, (4 * CAP, META), 0) // CAP
        lane = lax.broadcasted_iota(jnp.int32, (4 * CAP, META), 1)
        spots = jnp.where(slot_row < 2, near * 2 + slot_row, far * 2 + slot_row - 2)
        return (lane == z * PLANE + spots).astype(jnp.bfloat16)

    slot_row = lax.broadcasted_iota(jnp.int32, (PLANE * CAP, META), 0)
    lane = lax.broadcasted_iota(jnp.int32, (PLANE * CAP, META), 1)
    plane_hot = (lane == z * PLANE + slot_row // CAP).astype(jnp.bfloat16)
    own_hot = expert_hot(x, at_x(-1))
    side_hot = expert_hot(x, at_x(1))

    def placing(hot, meta):
        ranks = lax.dot_general(
            hot, meta, (((1,), (1,)), ((), ())), preferred_element_type=jnp.float32
        )
        wanted = lax.broadcasted_iota(jnp.int32, ranks.shape, 0) % CAP
        return (ranks == wanted.astype(jnp.float32)).astype(jnp.float32).astype(jnp.bfloat16)

    def slots(place, block):
        got = jnp.dot(place, block, preferred_element_type=jnp.float32)
        return got.reshape(place.shape[0] // CAP, CAP, block.shape[1])

    def compact_half(i, zz):
        place = placing(plane_hot, raw[zz, :, D:])
        for lo in range(0, HALF, 1024):
            both = jnp.concatenate(
                [
                    slots(place, raw[zz, :, lo : lo + 1024]),
                    slots(place, raw[zz, :, HALF + lo : HALF + lo + 1024]),
                ],
                axis=1,
            )
            half_out[i, :, :, lo : lo + 1024] = both.astype(jnp.bfloat16)

    def compact_pair(k, hot, source, meta_at, first, out, place_at):
        upper, lower = at_z(k), at_z(-k)
        place_u = placing(hot, source[upper, :, meta_at : meta_at + META])
        place_l = placing(hot, source[lower, :, meta_at : meta_at + META])
        for lo in range(0, HALF, 1024):
            both = jnp.concatenate(
                [
                    slots(place_u, source[upper, :, first + lo : first + lo + 1024]),
                    slots(place_l, source[lower, :, first + lo : first + lo + 1024]),
                ],
                axis=1,
            )
            rows = hot.shape[0] // CAP
            out[k - 1, place_at : place_at + rows, :, lo : lo + 1024] = both.astype(jnp.bfloat16)

    def plane_refs(chunk):
        if chunk in (0, 4):
            return half_out.at[chunk // 4], half_in.at[chunk // 4]
        return low_out.at[chunk - 1], low_in.at[chunk - 1]

    def plane_copy(chunk, o):
        outgoing, incoming = plane_refs(chunk)
        target = (spot + o) % PLANE
        return pltpu.make_async_remote_copy(
            src_ref=outgoing.at[target],
            dst_ref=incoming.at[spot],
            send_sem=p_send.at[chunk * PLANE + target],
            recv_sem=p_recv.at[chunk * PLANE + spot],
            device_id=dev(z, target),
            device_id_type=MESH,
        )

    def plane_own(chunk):
        outgoing, incoming = plane_refs(chunk)
        return pltpu.make_async_copy(
            outgoing.at[spot], incoming.at[spot], p_recv.at[chunk * PLANE + spot]
        )

    def plane_start(chunk):
        for o in range(1, PLANE):
            plane_copy(chunk, o).start()
        plane_own(chunk).start()

    def plane_wait(chunk):
        outgoing, incoming = plane_refs(chunk)
        for o in range(1, PLANE):
            source = (spot + o) % PLANE
            pltpu.make_async_remote_copy(
                src_ref=outgoing.at[source],
                dst_ref=incoming.at[source],
                send_sem=p_send.at[chunk * PLANE + source],
                recv_sem=p_recv.at[chunk * PLANE + source],
                device_id=dev(z, source),
                device_id_type=MESH,
            ).wait_recv()
        plane_own(chunk).wait()

    def high_copy(k, place, steps, other, origin):
        return pltpu.make_async_remote_copy(
            src_ref=high_out.at[k - 1, place],
            dst_ref=high_in.at[k - 1, origin],
            send_sem=h_send.at[(k - 1) * PLANE + place],
            recv_sem=h_recv.at[(k - 1) * PLANE + origin],
            device_id=dev(z, spot_of(steps, other)),
            device_id_type=MESH,
        )

    def high_local(k, place, origin):
        return pltpu.make_async_copy(
            high_out.at[k - 1, place],
            high_in.at[k - 1, origin],
            h_recv.at[(k - 1) * PLANE + origin],
        )

    def high_list(k, base, far, origin):
        return [
            high_copy(k, base + (core + 1) % 2, 0, 1, origin),
            high_copy(k, base + 2 + core, far, 0, origin),
            high_copy(k, base + 2 + (core + 1) % 2, far, 1, origin),
        ]

    def high_own(k):
        return high_list(k, 0, -1, spot)

    def high_side(k):
        return high_list(k, 4, 1, spot_of(-1, 0))

    def high_start(k, base, copies, origin):
        for copy in copies:
            copy.start()
        high_local(k, base + core, origin).start()

    def high_wait(k):
        for steps, other in ((1, 0), (2, 0), (0, 1), (1, 1), (2, 1), (3, 1)):
            high_copy(k, 0, 0, 1, spot_of(steps, other)).wait_recv()
        high_local(k, core, spot).wait()
        high_local(k, 4 + core, spot_of(-1, 0)).wait()

    def gated(gate_val, up_val):
        return gate_val / (1.0 + jnp.exp(-gate_val)) * up_val

    def give_back(values, dz_index):
        both = jnp.concatenate([values[:, :, : FFW // 2], values[:, :, FFW // 2 :]], axis=1)
        ret_out[dz_index] = both.astype(jnp.bfloat16)

    def ret_copy(dz, r):
        idx = (dz + NZ) % NZ
        return pltpu.make_async_remote_copy(
            src_ref=ret_out.at[idx, r],
            dst_ref=ret_in.at[ep],
            send_sem=r_send.at[idx * PLANE + r],
            recv_sem=r_recv.at[ep],
            device_id=dev(at_z(dz), r),
            device_id_type=MESH,
        )

    def ret_own():
        return pltpu.make_async_copy(ret_out.at[0, spot], ret_in.at[ep], r_recv.at[ep])

    def ret_start(dz):
        for o in range(PLANE):
            if dz == 0 and o == 0:
                ret_own().start()
            else:
                ret_copy(dz, (spot + o) % PLANE).start()

    def expert_half(chunk):
        plane_wait(chunk)
        for lo in range(0, FFW, 256):
            rows = half_in[chunk // 4].reshape(PLANE * 16, HALF)

            def halves(mat):
                first = jnp.dot(
                    rows, mat[:HALF, lo : lo + 256], preferred_element_type=jnp.float32
                ).reshape(PLANE, 16, 256)
                second = jnp.dot(
                    rows, mat[HALF:, lo : lo + 256], preferred_element_type=jnp.float32
                ).reshape(PLANE, 16, 256)
                return first[:, :CAP] + second[:, CAP:]

            act[:, :CAP, lo : lo + 256] = gated(halves(gate_w), halves(up_w))
        give_back(act[:, :CAP], chunk)
        ret_start(chunk)

    def expert_pair(k):
        plane_wait(k)
        high_wait(k)
        for lo in range(0, FFW, 256):
            low = low_in[k - 1].reshape(PLANE * 16, HALF)
            high = high_in[k - 1].reshape(PLANE * 16, HALF)

            def both(mat):
                return jnp.dot(
                    low, mat[:HALF, lo : lo + 256], preferred_element_type=jnp.float32
                ) + jnp.dot(high, mat[HALF:, lo : lo + 256], preferred_element_type=jnp.float32)

            act[:, :, lo : lo + 256] = gated(both(gate_w), both(up_w)).reshape(PLANE, 16, 256)
        give_back(act[:, :CAP], k)
        give_back(act[:, CAP:], NZ - k)
        ret_start(k)
        ret_start(-k)

    hop(1, 1).start()
    hop(-1, 1).start()
    side_first().start()
    compact_half(0, z)
    plane_start(0)
    pick_columns(ids_ref, scores_ref, rank, pos_col, share_col)
    side_copy(0, side.at[z], side.at[z], dev(z, spot_of(1, 0))).wait_recv()
    side_hop(1, 1).start()
    side_hop(-1, 1).start()
    for sign in (1, -1):
        arrived(sign, 1)
        hop(sign, 1 + 1).start()
    compact_pair(1, plane_hot, raw, D, 0, low_out, 0)
    plane_start(1)
    compact_pair(1, own_hot, raw, D, HALF, high_out, 0)
    high_start(1, 0, high_own(1), spot)
    for sign in (1, -1):
        side_arrived(sign, 1)
        side_hop(sign, 1 + 1).start()
    compact_pair(1, side_hot, side, HALF, 0, high_out, 4)
    high_start(1, 4, high_side(1), spot_of(-1, 0))
    for copy in w_copies:
        copy.wait()
    expert_half(0)
    for sign in (1, -1):
        arrived(sign, 2)
        hop(sign, 2 + 1).start()
    compact_pair(2, plane_hot, raw, D, 0, low_out, 0)
    plane_start(2)
    compact_pair(2, own_hot, raw, D, HALF, high_out, 0)
    high_start(2, 0, high_own(2), spot)
    for sign in (1, -1):
        side_arrived(sign, 2)
        side_hop(sign, 2 + 1).start()
    compact_pair(2, side_hot, side, HALF, 0, high_out, 4)
    high_start(2, 4, high_side(2), spot_of(-1, 0))
    expert_pair(1)
    for sign in (1, -1):
        arrived(sign, 3)
        hop(sign, 3 + 1).start()
    compact_pair(3, plane_hot, raw, D, 0, low_out, 0)
    plane_start(3)
    compact_pair(3, own_hot, raw, D, HALF, high_out, 0)
    high_start(3, 0, high_own(3), spot)
    expert_pair(2)
    for sign in (1, -1):
        side_arrived(sign, 3)
    compact_pair(3, side_hot, side, HALF, 0, high_out, 4)
    high_start(3, 4, high_side(3), spot_of(-1, 0))
    arrived(1, 4)
    arrived(-1, 4)
    compact_half(1, at_z(4))
    plane_start(4)
    expert_pair(3)
    expert_half(4)

    side_first().wait_send()
    for sign in (1, -1):
        for k in (1, 2, 3, 4):
            hop(sign, k).wait_send()
        for k in (1, 2, 3):
            side_hop(sign, k).wait_send()
    for k in (1, 2, 3):
        for copy in high_own(k) + high_side(k):
            copy.wait_send()
    for chunk in range(5):
        for o in range(1, PLANE):
            plane_copy(chunk, o).wait_send()

    def ret_sent(i, carry):
        dz_index = i // PLANE
        pltpu.make_async_remote_copy(
            src_ref=ret_out.at[dz_index, i % PLANE],
            dst_ref=ret_in.at[ep],
            send_sem=r_send.at[i],
            recv_sem=r_recv.at[ep],
            device_id=dev(at_z(dz_index), i % PLANE),
            device_id_type=MESH,
        ).wait_send()
        return carry

    for o in range(1, PLANE):
        ret_copy(0, (spot + o) % PLANE).wait_send()
    lax.fori_loop(PLANE, NZ * PLANE, ret_sent, 0)

    def ret_got(o, carry):
        expert = (ep + o) % (NZ * PLANE)
        pltpu.make_async_remote_copy(
            src_ref=ret_in.at[expert],
            dst_ref=ret_in.at[expert],
            send_sem=r_send.at[o],
            recv_sem=r_recv.at[expert],
            device_id={"ep": expert},
            device_id_type=MESH,
        ).wait_recv()
        return carry

    ret_own().wait()
    lax.fori_loop(1, NZ * PLANE, ret_got, 0)

    back = ret_in[...].reshape(NZ * PLANE * 16, FFW // 2)
    column = lax.broadcasted_iota(jnp.int32, (TOK * 8, NZ * PLANE * 16), 1)
    for half in (0, 1):
        pick = (column == pos_col[...] + CAP * half).astype(jnp.float32).astype(jnp.bfloat16)
        got = jnp.dot(pick, back, preferred_element_type=jnp.float32)
        out_ref[:, half * (FFW // 2) : (half + 1) * (FFW // 2)] = (
            share_col[...] * got
        ).astype(jnp.bfloat16)


def layer_call(*args):
    bf = jnp.bfloat16
    dma = pltpu.SemaphoreType.DMA
    vmem = pl.BlockSpec(memory_space=pltpu.VMEM)
    hbm = pl.BlockSpec(memory_space=pl.ANY)
    return pl.pallas_call(
        layer_kernel,
        out_shape=(
            jax.ShapeDtypeStruct((TOK * 8, FFW), bf),
            jax.ShapeDtypeStruct((TOK, D), bf),
        ),
        in_specs=[hbm] * 12,
        out_specs=(vmem, vmem),
        scratch_shapes=[
            pltpu.VMEM((TOK, D), bf),
            pltpu.VMEM((1, D), jnp.float32),
            pltpu.VMEM((8, TOK), jnp.int32),
            pltpu.VMEM((8, TOK), jnp.float32),
            pltpu.VMEM((TOK, D), bf),
            pltpu.VMEM((TOK, 16, 2 * HD), bf),
            pltpu.VMEM((TOK, 16, 2 * HD), bf),
            pltpu.VMEM((TOK, 2 * HD), bf),
            pltpu.VMEM((TOK, 2 * HD), bf),
            pltpu.VMEM((1, TOK), jnp.int32),
            pltpu.VMEM((NZ, TOK, D + META), bf),
            pltpu.VMEM((NZ, TOK, HALF + META), bf),
            pltpu.VMEM((2, PLANE, 16, HALF), bf),
            pltpu.VMEM((3, PLANE, 16, HALF), bf),
            pltpu.VMEM((3, PLANE, 16, HALF), bf),
            pltpu.VMEM((2, PLANE, 16, HALF), bf),
            pltpu.VMEM((3, PLANE, 16, HALF), bf),
            pltpu.VMEM((3, PLANE, 16, HALF), bf),
            pltpu.VMEM((D, FFW), bf),
            pltpu.VMEM((D, FFW), bf),
            pltpu.VMEM((PLANE, 16, FFW), jnp.float32),
            pltpu.VMEM((NZ, PLANE, 16, FFW // 2), bf),
            pltpu.VMEM((NZ * PLANE, 16, FFW // 2), bf),
            pltpu.VMEM((TOK * 8, 1), jnp.int32),
            pltpu.VMEM((TOK * 8, 1), jnp.float32),
            dma((10,)),
            dma((2,)),
            dma((8,)),
            dma((8,)),
            dma((7,)),
            dma((7,)),
            dma((5 * PLANE,)),
            dma((5 * PLANE,)),
            dma((3 * PLANE,)),
            dma((3 * PLANE,)),
            dma((NZ * PLANE,)),
            dma((NZ * PLANE,)),
        ],
        compiler_params=pltpu.CompilerParams(
            collective_id=0, has_side_effects=True, vmem_limit_bytes=60 * 1024 * 1024
        ),
        cost_estimate=pl.CostEstimate(
            flops=2 * 512 * D * 2 * FFW, bytes_accessed=2 * D * FFW * 2, transcendentals=512 * FFW
        ),
    )(*args)


def hand_over_kernel(terms_in, attended_in, terms_out, attended_out, terms_buf, attended_buf, sem):
    arriving, leaving = [], []
    for source, middle, target in (
        (terms_in, terms_buf, terms_out),
        (attended_in, attended_buf, attended_out),
    ):
        step = source.shape[0] // 2
        for part in range(2):
            rows = pl.ds(part * step, step)
            i = 2 * len(arriving)
            arriving.append(pltpu.make_async_copy(source.at[rows], middle.at[rows], sem.at[i]))
            leaving.append(pltpu.make_async_copy(middle.at[rows], target.at[rows], sem.at[i + 1]))
    for copy in arriving:
        copy.start()
    for first, second in zip(arriving, leaving):
        first.wait()
        second.start()
    for copy in leaving:
        copy.wait()


def hand_over(terms, attended):
    hbm = pl.BlockSpec(memory_space=pl.ANY)
    return pl.pallas_call(
        hand_over_kernel,
        out_shape=(
            jax.ShapeDtypeStruct(terms.shape, terms.dtype),
            jax.ShapeDtypeStruct(attended.shape, attended.dtype),
        ),
        in_specs=[hbm, hbm],
        out_specs=(hbm, hbm),
        scratch_shapes=[
            pltpu.VMEM(terms.shape, terms.dtype),
            pltpu.VMEM(attended.shape, attended.dtype),
            pltpu.SemaphoreType.DMA((8,)),
        ],
        compiler_params=pltpu.CompilerParams(vmem_limit_bytes=60 * 1024 * 1024),
    )(terms, attended)


def local(
    tokens,
    norm_gain,
    gate_weight,
    up_weight,
    route_ids,
    route_scores,
    queries,
    key_cache,
    value_cache,
    new_keys,
    new_values,
    cache_lengths,
):
    expert_terms, attended = layer_call(
        tokens,
        norm_gain.reshape(1, -1),
        gate_weight,
        up_weight,
        route_ids.T,
        route_scores.T,
        queries,
        key_cache,
        value_cache,
        new_keys,
        new_values,
        cache_lengths.reshape(1, -1),
    )
    expert_terms, attended = hand_over(expert_terms, attended)
    return (expert_terms.reshape(route_ids.shape[0], route_ids.shape[1], FFW), attended)


def solution(mesh):
    return jax.shard_map(
        local,
        mesh=mesh,
        in_specs=(
            P(("rep", "ep"), None),
            P(),
            P(("rep", "ep"), None, None),
            P(("rep", "ep"), None, None),
            P(("rep", "ep"), None),
            P(("rep", "ep"), None),
            P(("rep", "ep"), None),
            P(("rep", "ep"), None, None),
            P(("rep", "ep"), None, None),
            P(("rep", "ep"), None),
            P(("rep", "ep"), None),
            P(("rep", "ep")),
        ),
        out_specs=(P(("rep", "ep"), None, None), P(("rep", "ep"), None)),
        check_vma=False,
    )
```

```python
import jax
import jax.experimental.pallas as pl
import jax.experimental.pallas.tpu as pltpu
import jax.numpy as jnp
from jax import lax
from jax.sharding import PartitionSpec as P

HD = 128
D = 4096
FFW = 768
TOK = 32
CAP = 8
NZ = 8
PLANE = 8
META = 128
HALF = D // 2
MESH = pl.DeviceIdType.MESH


def attend_rows(
    queries_ref, keys_ref, values_ref, new_keys_ref, new_values_ref, lengths_ref, attended_ref
):
    rows, heads = 16, 16
    size = rows * heads
    row = lax.broadcasted_iota(jnp.int32, (size, size), 0) % rows
    lane = lax.broadcasted_iota(jnp.int32, (size, size), 1)
    own_row = lax.broadcasted_iota(jnp.int32, (size, rows), 0) % rows
    own_lane = lax.broadcasted_iota(jnp.int32, (size, rows), 1)
    factor = HD ** (-0.5)
    contract = (((1,), (1,)), ((), ()))
    for first in range(0, TOK, rows):
        part = slice(first, first + rows)
        repeat = (
            lax.broadcasted_iota(jnp.int32, (TOK, size), 0)
            == first + lax.broadcasted_iota(jnp.int32, (TOK, size), 1) // rows
        ).astype(jnp.float32)
        counts = jnp.broadcast_to(lengths_ref[...].astype(jnp.float32), (8, TOK))
        lengths = jnp.dot(counts, repeat, preferred_element_type=jnp.float32)[:1]
        live = (row == lane // rows) & ((lane % rows).astype(jnp.float32) < lengths)
        for kv in range(2):
            cols = slice(kv * HD, (kv + 1) * HD)
            query = jnp.concatenate(
                [
                    queries_ref[part, (kv * heads + g) * HD : (kv * heads + g + 1) * HD]
                    for g in range(heads)
                ],
                axis=0,
            )
            key = keys_ref[part, :, cols].reshape(size, HD)
            value = values_ref[part, :, cols].reshape(size, HD)
            scores = factor * lax.dot_general(
                query, key, contract, preferred_element_type=jnp.float32
            )
            scores = jnp.where(live, scores, -1e30)
            own = factor * lax.dot_general(
                query, new_keys_ref[part, cols], contract, preferred_element_type=jnp.float32
            )
            own = jnp.sum(jnp.where(own_row == own_lane, own, 0.0), axis=1, keepdims=True)
            top = jnp.maximum(jnp.max(scores, axis=1, keepdims=True), own)
            weights = jnp.where(live, jnp.exp(scores - top), 0.0)
            own_weight = jnp.exp(own - top)
            mass = jnp.sum(weights, axis=1, keepdims=True) + own_weight
            probs = (weights / mass).astype(jnp.bfloat16)
            own_prob = (own_weight / mass).astype(jnp.bfloat16).astype(jnp.float32)
            fresh = jnp.concatenate(
                [new_values_ref[part, cols].astype(jnp.float32)] * heads, axis=0
            )
            summed = jnp.dot(probs, value, preferred_element_type=jnp.float32) + own_prob * fresh
            for g in range(heads):
                attended_ref[part, (kv * heads + g) * HD : (kv * heads + g + 1) * HD] = summed[
                    g * rows : (g + 1) * rows
                ].astype(jnp.bfloat16)


def norm_rows(tokens_ref, attended_ref, gain_ref, rows_ref):
    step = 1024
    total = jnp.zeros((TOK, 1), jnp.float32)
    for lo in range(0, D, step):
        cols = slice(lo, lo + step)
        hidden = tokens_ref[:, cols].astype(jnp.float32) + attended_ref[:, cols].astype(
            jnp.float32
        )
        hidden = hidden.astype(jnp.bfloat16)
        rows_ref[:, cols] = hidden
        hidden = hidden.astype(jnp.float32)
        total = total + jnp.sum(hidden * hidden, axis=1, keepdims=True)
    scale = lax.rsqrt(total / D + 1e-06)
    for lo in range(0, D, step):
        cols = slice(lo, lo + step)
        hidden = rows_ref[:, cols].astype(jnp.float32)
        rows_ref[:, cols] = (hidden * scale * gain_ref[:, cols]).astype(jnp.bfloat16)


def slot_ranks(ids_ref):
    expert = lax.broadcasted_iota(jnp.int32, (META, TOK), 0)
    hit = jnp.zeros((META, TOK), jnp.float32)
    for k in range(8):
        hit = hit + (expert == ids_ref[k : k + 1, :]).astype(jnp.float32)
    row = lax.broadcasted_iota(jnp.int32, (TOK, TOK), 0)
    col = lax.broadcasted_iota(jnp.int32, (TOK, TOK), 1)
    hit = hit.astype(jnp.bfloat16)

    def over_rows(mat):
        return lax.dot_general(
            mat.astype(jnp.float32).astype(jnp.bfloat16),
            hit,
            (((1,), (1,)), ((), ())),
            preferred_element_type=jnp.float32,
        )

    by_expert = jnp.dot(
        hit,
        (row < col).astype(jnp.float32).astype(jnp.bfloat16),
        preferred_element_type=jnp.float32,
    )
    meta = jnp.where(over_rows(row == col) > 0.0, over_rows(row > col), -1.0)
    return meta.astype(jnp.bfloat16), by_expert


def pick_columns(ids_ref, scores_ref, rank, pos_col, share_col):
    expert = lax.broadcasted_iota(jnp.int32, (META, TOK), 0)
    slot = jnp.concatenate(
        [
            jnp.sum(jnp.where(expert == ids_ref[k : k + 1, :], rank, 0.0), axis=0, keepdims=True)
            for k in range(8)
        ],
        axis=0,
    )
    score = scores_ref[...]
    share = score / jnp.sum(score, axis=0, keepdims=True)
    spread = (
        lax.broadcasted_iota(jnp.int32, (TOK * 8, TOK), 0) // 8
        == lax.broadcasted_iota(jnp.int32, (TOK * 8, TOK), 1)
    ).astype(jnp.float32)
    mine = lax.broadcasted_iota(jnp.int32, (TOK * 8, 8), 0) % 8 == lax.broadcasted_iota(
        jnp.int32, (TOK * 8, 8), 1
    )

    def column(values):
        every = lax.dot_general(
            spread,
            values,
            (((1,), (1,)), ((), ())),
            precision=lax.Precision.HIGHEST,
            preferred_element_type=jnp.float32,
        )
        return jnp.sum(jnp.where(mine, every, 0.0), axis=1, keepdims=True)

    pos_col[...] = column(ids_ref[...].astype(jnp.float32) * 16.0 + slot).astype(jnp.int32)
    share_col[...] = column(share)


def layer_kernel(
    tokens_hbm, gain_hbm, gate_hbm, up_hbm, ids_hbm, scores_hbm, queries_hbm, keys_hbm,
    values_hbm, new_keys_hbm, new_values_hbm, lengths_hbm, out_ref, attended_ref,
    tokens_ref, gain_ref, ids_ref, scores_ref, queries_ref, keys_ref,
    values_ref, new_keys_ref, new_values_ref, lengths_ref,
    raw, side, half_out, low_out, high_out, half_in, low_in, high_in,
    gate_w, up_w, act, ret_out, ret_in, pos_col, share_col, picked,
    in_sem, w_sem, z_send, z_recv, n_send, n_recv, p_send, p_recv, h_send, h_recv, r_send, r_recv,
):
    ep = lax.axis_index("ep")
    z = ep // PLANE
    spot = ep % PLANE
    x = spot // 2
    core = spot % 2
    turn = 1 - 2 * core

    def at_x(steps):
        return (x + steps * turn + 4) % 4

    def spot_of(steps, other):
        return at_x(steps) * 2 + (core + other) % 2

    def at_z(dz):
        return (z + dz + NZ) % NZ

    def dev(zz, ss):
        return {"ep": zz * PLANE + ss}

    in_copies = [
        pltpu.make_async_copy(source, target, in_sem.at[i])
        for i, (source, target) in enumerate(
            (
                (queries_hbm, queries_ref),
                (keys_hbm, keys_ref),
                (values_hbm, values_ref),
                (new_keys_hbm, new_keys_ref),
                (new_values_hbm, new_values_ref),
                (lengths_hbm, lengths_ref),
                (tokens_hbm, tokens_ref),
                (gain_hbm, gain_ref),
                (ids_hbm, ids_ref),
                (scores_hbm, scores_ref),
            )
        )
    ]
    w_copies = [
        pltpu.make_async_copy(gate_hbm.at[0], gate_w, w_sem.at[0]),
        pltpu.make_async_copy(up_hbm.at[0], up_w, w_sem.at[1]),
    ]
    for copy in in_copies + w_copies:
        copy.start()
    barrier = pltpu.get_barrier_semaphore()

    for sign in (1, -1):
        pl.semaphore_signal(barrier, inc=1, device_id=dev(at_z(sign), spot), device_id_type=MESH)
    for o in range(1, PLANE):
        pl.semaphore_signal(
            barrier, inc=1, device_id=dev(z, (spot + o) % PLANE), device_id_type=MESH
        )
    for copy in in_copies:
        copy.wait()
    attend_rows(
        queries_ref, keys_ref, values_ref, new_keys_ref, new_values_ref, lengths_ref, attended_ref
    )
    norm_rows(tokens_ref, attended_ref, gain_ref, raw.at[z])
    meta, rank = slot_ranks(ids_ref)
    raw[z, :, D:] = meta
    pl.semaphore_wait(barrier, PLANE + 1)

    def hop(sign, k):
        block = raw.at[at_z(-sign * (k - 1))]
        if k == 4:
            block = block.at[pl.ds(0 if sign > 0 else 16, 16)]
        idx = (k - 1) + (0 if sign > 0 else 4)
        return pltpu.make_async_remote_copy(
            src_ref=block,
            dst_ref=block,
            send_sem=z_send.at[idx],
            recv_sem=z_recv.at[idx],
            device_id=dev(at_z(sign), spot),
            device_id_type=MESH,
        )

    def arrived(sign, k):
        block = raw.at[at_z(-sign * k)]
        if k == 4:
            block = block.at[pl.ds(0 if sign > 0 else 16, 16)]
        idx = (k - 1) + (0 if sign > 0 else 4)
        pltpu.make_async_remote_copy(
            src_ref=block,
            dst_ref=block,
            send_sem=z_send.at[idx],
            recv_sem=z_recv.at[idx],
            device_id=dev(at_z(sign), spot),
            device_id_type=MESH,
        ).wait_recv()

    def side_copy(idx, block_out, block_in, device):
        return pltpu.make_async_remote_copy(
            src_ref=block_out,
            dst_ref=block_in,
            send_sem=n_send.at[idx],
            recv_sem=n_recv.at[idx],
            device_id=device,
            device_id_type=MESH,
        )

    def side_first():
        return side_copy(
            0, raw.at[z, :, pl.ds(HALF, HALF + META)], side.at[z], dev(z, spot_of(1, 0))
        )

    def side_hop(sign, k):
        block = side.at[at_z(-sign * (k - 1))]
        return side_copy(k if sign > 0 else k + 3, block, block, dev(at_z(sign), spot))

    def side_arrived(sign, k):
        block = side.at[at_z(-sign * k)]
        side_copy(k if sign > 0 else k + 3, block, block, dev(at_z(sign), spot)).wait_recv()

    def expert_hot(near, far):
        slot_row = lax.broadcasted_iota(jnp.int32, (4 * CAP, META), 0) // CAP
        lane = lax.broadcasted_iota(jnp.int32, (4 * CAP, META), 1)
        spots = jnp.where(slot_row < 2, near * 2 + slot_row, far * 2 + slot_row - 2)
        return (lane == z * PLANE + spots).astype(jnp.bfloat16)

    slot_row = lax.broadcasted_iota(jnp.int32, (PLANE * CAP, META), 0)
    lane = lax.broadcasted_iota(jnp.int32, (PLANE * CAP, META), 1)
    plane_hot = (lane == z * PLANE + slot_row // CAP).astype(jnp.bfloat16)
    own_hot = expert_hot(x, at_x(-1))
    side_hot = expert_hot(x, at_x(1))

    def placing(hot, meta):
        ranks = lax.dot_general(
            hot, meta, (((1,), (1,)), ((), ())), preferred_element_type=jnp.float32
        )
        wanted = lax.broadcasted_iota(jnp.int32, ranks.shape, 0) % CAP
        return (ranks == wanted.astype(jnp.float32)).astype(jnp.float32).astype(jnp.bfloat16)

    def slots(place, block):
        got = jnp.dot(place, block, preferred_element_type=jnp.float32)
        return got.reshape(place.shape[0] // CAP, CAP, block.shape[1])

    def compact_half(i, zz):
        place = placing(plane_hot, raw[zz, :, D:])
        for lo in range(0, HALF, 1024):
            both = jnp.concatenate(
                [
                    slots(place, raw[zz, :, lo : lo + 1024]),
                    slots(place, raw[zz, :, HALF + lo : HALF + lo + 1024]),
                ],
                axis=1,
            )
            half_out[i, :, :, lo : lo + 1024] = both.astype(jnp.bfloat16)

    def compact_pair(k, hot, source, meta_at, first, out, place_at):
        upper, lower = at_z(k), at_z(-k)
        place_u = placing(hot, source[upper, :, meta_at : meta_at + META])
        place_l = placing(hot, source[lower, :, meta_at : meta_at + META])
        for lo in range(0, HALF, 1024):
            both = jnp.concatenate(
                [
                    slots(place_u, source[upper, :, first + lo : first + lo + 1024]),
                    slots(place_l, source[lower, :, first + lo : first + lo + 1024]),
                ],
                axis=1,
            )
            rows = hot.shape[0] // CAP
            out[k - 1, place_at : place_at + rows, :, lo : lo + 1024] = both.astype(jnp.bfloat16)

    def plane_refs(chunk):
        if chunk in (0, 4):
            return half_out.at[chunk // 4], half_in.at[chunk // 4]
        return low_out.at[chunk - 1], low_in.at[chunk - 1]

    def plane_copy(chunk, o):
        outgoing, incoming = plane_refs(chunk)
        target = (spot + o) % PLANE
        return pltpu.make_async_remote_copy(
            src_ref=outgoing.at[target],
            dst_ref=incoming.at[spot],
            send_sem=p_send.at[chunk * PLANE + target],
            recv_sem=p_recv.at[chunk * PLANE + spot],
            device_id=dev(z, target),
            device_id_type=MESH,
        )

    def plane_own(chunk):
        outgoing, incoming = plane_refs(chunk)
        return pltpu.make_async_copy(
            outgoing.at[spot], incoming.at[spot], p_recv.at[chunk * PLANE + spot]
        )

    def plane_start(chunk):
        for o in range(1, PLANE):
            plane_copy(chunk, o).start()
        plane_own(chunk).start()

    def plane_wait(chunk):
        outgoing, incoming = plane_refs(chunk)
        for o in range(1, PLANE):
            source = (spot + o) % PLANE
            pltpu.make_async_remote_copy(
                src_ref=outgoing.at[source],
                dst_ref=incoming.at[source],
                send_sem=p_send.at[chunk * PLANE + source],
                recv_sem=p_recv.at[chunk * PLANE + source],
                device_id=dev(z, source),
                device_id_type=MESH,
            ).wait_recv()
        plane_own(chunk).wait()

    def high_copy(k, place, steps, other, origin):
        return pltpu.make_async_remote_copy(
            src_ref=high_out.at[k - 1, place],
            dst_ref=high_in.at[k - 1, origin],
            send_sem=h_send.at[(k - 1) * PLANE + place],
            recv_sem=h_recv.at[(k - 1) * PLANE + origin],
            device_id=dev(z, spot_of(steps, other)),
            device_id_type=MESH,
        )

    def high_local(k, place, origin):
        return pltpu.make_async_copy(
            high_out.at[k - 1, place],
            high_in.at[k - 1, origin],
            h_recv.at[(k - 1) * PLANE + origin],
        )

    def high_list(k, base, far, origin):
        return [
            high_copy(k, base + (core + 1) % 2, 0, 1, origin),
            high_copy(k, base + 2 + core, far, 0, origin),
            high_copy(k, base + 2 + (core + 1) % 2, far, 1, origin),
        ]

    def high_own(k):
        return high_list(k, 0, -1, spot)

    def high_side(k):
        return high_list(k, 4, 1, spot_of(-1, 0))

    def high_start(k, base, copies, origin):
        for copy in copies:
            copy.start()
        high_local(k, base + core, origin).start()

    def high_wait(k):
        for steps, other in ((1, 0), (2, 0), (0, 1), (1, 1), (2, 1), (3, 1)):
            high_copy(k, 0, 0, 1, spot_of(steps, other)).wait_recv()
        high_local(k, core, spot).wait()
        high_local(k, 4 + core, spot_of(-1, 0)).wait()

    def gated(gate_val, up_val):
        return gate_val / (1.0 + jnp.exp(-gate_val)) * up_val

    def give_back(values, dz_index):
        both = jnp.concatenate([values[:, :, : FFW // 2], values[:, :, FFW // 2 :]], axis=1)
        ret_out[dz_index] = both.astype(jnp.bfloat16)

    def ret_copy(dz, r):
        idx = (dz + NZ) % NZ
        return pltpu.make_async_remote_copy(
            src_ref=ret_out.at[idx, r],
            dst_ref=ret_in.at[ep],
            send_sem=r_send.at[idx * PLANE + r],
            recv_sem=r_recv.at[ep],
            device_id=dev(at_z(dz), r),
            device_id_type=MESH,
        )

    def ret_own():
        return pltpu.make_async_copy(ret_out.at[0, spot], ret_in.at[ep], r_recv.at[ep])

    def ret_start(dz):
        for o in range(PLANE):
            if dz == 0 and o == 0:
                ret_own().start()
            else:
                ret_copy(dz, (spot + o) % PLANE).start()

    def expert_half(chunk):
        plane_wait(chunk)
        for lo in range(0, FFW, 256):
            rows = half_in[chunk // 4].reshape(PLANE * 16, HALF)

            def halves(mat):
                first = jnp.dot(
                    rows, mat[:HALF, lo : lo + 256], preferred_element_type=jnp.float32
                ).reshape(PLANE, 16, 256)
                second = jnp.dot(
                    rows, mat[HALF:, lo : lo + 256], preferred_element_type=jnp.float32
                ).reshape(PLANE, 16, 256)
                return first[:, :CAP] + second[:, CAP:]

            act[:, :CAP, lo : lo + 256] = gated(halves(gate_w), halves(up_w))
        give_back(act[:, :CAP], chunk)
        ret_start(chunk)

    def expert_pair(k):
        plane_wait(k)
        high_wait(k)
        for lo in range(0, FFW, 256):
            low = low_in[k - 1].reshape(PLANE * 16, HALF)
            high = high_in[k - 1].reshape(PLANE * 16, HALF)

            def both(mat):
                return jnp.dot(
                    low, mat[:HALF, lo : lo + 256], preferred_element_type=jnp.float32
                ) + jnp.dot(high, mat[HALF:, lo : lo + 256], preferred_element_type=jnp.float32)

            act[:, :, lo : lo + 256] = gated(both(gate_w), both(up_w)).reshape(PLANE, 16, 256)
        give_back(act[:, :CAP], k)
        give_back(act[:, CAP:], NZ - k)
        ret_start(k)
        ret_start(-k)

    hop(1, 1).start()
    hop(-1, 1).start()
    side_first().start()
    compact_half(0, z)
    plane_start(0)
    pick_columns(ids_ref, scores_ref, rank, pos_col, share_col)
    side_copy(0, side.at[z], side.at[z], dev(z, spot_of(1, 0))).wait_recv()
    side_hop(1, 1).start()
    side_hop(-1, 1).start()
    for sign in (1, -1):
        arrived(sign, 1)
        hop(sign, 1 + 1).start()
    compact_pair(1, plane_hot, raw, D, 0, low_out, 0)
    plane_start(1)
    compact_pair(1, own_hot, raw, D, HALF, high_out, 0)
    high_start(1, 0, high_own(1), spot)
    for sign in (1, -1):
        side_arrived(sign, 1)
        side_hop(sign, 1 + 1).start()
    compact_pair(1, side_hot, side, HALF, 0, high_out, 4)
    high_start(1, 4, high_side(1), spot_of(-1, 0))
    for copy in w_copies:
        copy.wait()
    expert_half(0)
    for sign in (1, -1):
        arrived(sign, 2)
        hop(sign, 2 + 1).start()
    compact_pair(2, plane_hot, raw, D, 0, low_out, 0)
    plane_start(2)
    compact_pair(2, own_hot, raw, D, HALF, high_out, 0)
    high_start(2, 0, high_own(2), spot)
    for sign in (1, -1):
        side_arrived(sign, 2)
        side_hop(sign, 2 + 1).start()
    compact_pair(2, side_hot, side, HALF, 0, high_out, 4)
    high_start(2, 4, high_side(2), spot_of(-1, 0))
    expert_pair(1)
    for sign in (1, -1):
        arrived(sign, 3)
        hop(sign, 3 + 1).start()
    compact_pair(3, plane_hot, raw, D, 0, low_out, 0)
    plane_start(3)
    compact_pair(3, own_hot, raw, D, HALF, high_out, 0)
    high_start(3, 0, high_own(3), spot)
    expert_pair(2)
    for sign in (1, -1):
        side_arrived(sign, 3)
    compact_pair(3, side_hot, side, HALF, 0, high_out, 4)
    high_start(3, 4, high_side(3), spot_of(-1, 0))
    arrived(1, 4)
    arrived(-1, 4)
    compact_half(1, at_z(4))
    plane_start(4)
    expert_pair(3)
    expert_half(4)

    def ret_got(o, plane):
        expert = plane * PLANE + (spot + o) % PLANE
        pltpu.make_async_remote_copy(
            src_ref=ret_in.at[expert],
            dst_ref=ret_in.at[expert],
            send_sem=r_send.at[o],
            recv_sem=r_recv.at[expert],
            device_id=dev((plane + 1) % NZ, spot),
            device_id_type=MESH,
        ).wait_recv()
        return plane

    column = lax.broadcasted_iota(jnp.int32, (TOK * 8, PLANE * 16), 1)

    def gather(planes, last):
        for dz in planes:
            if dz == 0:
                ret_own().wait()
            lax.fori_loop(1 if dz == 0 else 0, PLANE, ret_got, at_z(dz))
        for half in (0, 1):
            cols = slice(half * (FFW // 2), (half + 1) * (FFW // 2))
            got = jnp.zeros((TOK * 8, FFW // 2), jnp.float32)
            for dz in planes:
                base = at_z(dz) * PLANE * 16 - CAP * half
                pick = (column + base == pos_col[...]).astype(jnp.float32).astype(jnp.bfloat16)
                back = ret_in[pl.ds(at_z(dz) * PLANE, PLANE)].reshape(PLANE * 16, FFW // 2)
                got = got + jnp.dot(pick, back, preferred_element_type=jnp.float32)
            if last:
                got = share_col[...] * (picked[:, cols] + got)
                out_ref[:, cols] = got.astype(jnp.bfloat16)
            else:
                picked[:, cols] = got

    far_planes = (3, -3, 4)
    gather((0, 1, -1, 2, -2), False)
    side_first().wait_send()
    for sign in (1, -1):
        for k in (1, 2, 3, 4):
            hop(sign, k).wait_send()
        for k in (1, 2, 3):
            side_hop(sign, k).wait_send()
    for k in (1, 2, 3):
        for copy in high_own(k) + high_side(k):
            copy.wait_send()
    for chunk in range(5):
        for o in range(1, PLANE):
            plane_copy(chunk, o).wait_send()

    def ret_sent(i, carry):
        dz_index = i // PLANE
        pltpu.make_async_remote_copy(
            src_ref=ret_out.at[dz_index, i % PLANE],
            dst_ref=ret_in.at[ep],
            send_sem=r_send.at[i],
            recv_sem=r_recv.at[ep],
            device_id=dev(at_z(dz_index), i % PLANE),
            device_id_type=MESH,
        ).wait_send()
        return carry

    for o in range(1, PLANE):
        ret_copy(0, (spot + o) % PLANE).wait_send()
    lax.fori_loop(PLANE, NZ * PLANE, ret_sent, 0)

    gather(far_planes, True)


def layer_call(*args):
    bf = jnp.bfloat16
    dma = pltpu.SemaphoreType.DMA
    vmem = pl.BlockSpec(memory_space=pltpu.VMEM)
    hbm = pl.BlockSpec(memory_space=pl.ANY)
    return pl.pallas_call(
        layer_kernel,
        out_shape=(
            jax.ShapeDtypeStruct((TOK * 8, FFW), bf),
            jax.ShapeDtypeStruct((TOK, D), bf),
        ),
        in_specs=[hbm] * 12,
        out_specs=(vmem, vmem),
        scratch_shapes=[
            pltpu.VMEM((TOK, D), bf),
            pltpu.VMEM((1, D), jnp.float32),
            pltpu.VMEM((8, TOK), jnp.int32),
            pltpu.VMEM((8, TOK), jnp.float32),
            pltpu.VMEM((TOK, D), bf),
            pltpu.VMEM((TOK, 16, 2 * HD), bf),
            pltpu.VMEM((TOK, 16, 2 * HD), bf),
            pltpu.VMEM((TOK, 2 * HD), bf),
            pltpu.VMEM((TOK, 2 * HD), bf),
            pltpu.VMEM((1, TOK), jnp.int32),
            pltpu.VMEM((NZ, TOK, D + META), bf),
            pltpu.VMEM((NZ, TOK, HALF + META), bf),
            pltpu.VMEM((2, PLANE, 16, HALF), bf),
            pltpu.VMEM((3, PLANE, 16, HALF), bf),
            pltpu.VMEM((3, PLANE, 16, HALF), bf),
            pltpu.VMEM((2, PLANE, 16, HALF), bf),
            pltpu.VMEM((3, PLANE, 16, HALF), bf),
            pltpu.VMEM((3, PLANE, 16, HALF), bf),
            pltpu.VMEM((D, FFW), bf),
            pltpu.VMEM((D, FFW), bf),
            pltpu.VMEM((PLANE, 16, FFW), jnp.float32),
            pltpu.VMEM((NZ, PLANE, 16, FFW // 2), bf),
            pltpu.VMEM((NZ * PLANE, 16, FFW // 2), bf),
            pltpu.VMEM((TOK * 8, 1), jnp.int32),
            pltpu.VMEM((TOK * 8, 1), jnp.float32),
            pltpu.VMEM((TOK * 8, FFW), jnp.float32),
            dma((10,)),
            dma((2,)),
            dma((8,)),
            dma((8,)),
            dma((7,)),
            dma((7,)),
            dma((5 * PLANE,)),
            dma((5 * PLANE,)),
            dma((3 * PLANE,)),
            dma((3 * PLANE,)),
            dma((NZ * PLANE,)),
            dma((NZ * PLANE,)),
        ],
        compiler_params=pltpu.CompilerParams(
            collective_id=0, has_side_effects=True, vmem_limit_bytes=60 * 1024 * 1024
        ),
        cost_estimate=pl.CostEstimate(
            flops=2 * 512 * D * 2 * FFW, bytes_accessed=2 * D * FFW * 2, transcendentals=512 * FFW
        ),
    )(*args)


def hand_over_kernel(terms_in, attended_in, terms_out, attended_out, terms_buf, attended_buf, sem):
    arriving, leaving = [], []
    for source, middle, target in (
        (terms_in, terms_buf, terms_out),
        (attended_in, attended_buf, attended_out),
    ):
        step = source.shape[0] // 2
        for part in range(2):
            rows = pl.ds(part * step, step)
            i = 2 * len(arriving)
            arriving.append(pltpu.make_async_copy(source.at[rows], middle.at[rows], sem.at[i]))
            leaving.append(pltpu.make_async_copy(middle.at[rows], target.at[rows], sem.at[i + 1]))
    for copy in arriving:
        copy.start()
    for first, second in zip(arriving, leaving):
        first.wait()
        second.start()
    for copy in leaving:
        copy.wait()


def hand_over(terms, attended):
    hbm = pl.BlockSpec(memory_space=pl.ANY)
    return pl.pallas_call(
        hand_over_kernel,
        out_shape=(
            jax.ShapeDtypeStruct(terms.shape, terms.dtype),
            jax.ShapeDtypeStruct(attended.shape, attended.dtype),
        ),
        in_specs=[hbm, hbm],
        out_specs=(hbm, hbm),
        scratch_shapes=[
            pltpu.VMEM(terms.shape, terms.dtype),
            pltpu.VMEM(attended.shape, attended.dtype),
            pltpu.SemaphoreType.DMA((8,)),
        ],
        compiler_params=pltpu.CompilerParams(vmem_limit_bytes=60 * 1024 * 1024),
    )(terms, attended)


def local(
    tokens,
    norm_gain,
    gate_weight,
    up_weight,
    route_ids,
    route_scores,
    queries,
    key_cache,
    value_cache,
    new_keys,
    new_values,
    cache_lengths,
):
    expert_terms, attended = layer_call(
        tokens,
        norm_gain.reshape(1, -1),
        gate_weight,
        up_weight,
        route_ids.T,
        route_scores.T,
        queries,
        key_cache,
        value_cache,
        new_keys,
        new_values,
        cache_lengths.reshape(1, -1),
    )
    expert_terms, attended = hand_over(expert_terms, attended)
    return (expert_terms.reshape(route_ids.shape[0], route_ids.shape[1], FFW), attended)


def solution(mesh):
    return jax.shard_map(
        local,
        mesh=mesh,
        in_specs=(
            P(("rep", "ep"), None),
            P(),
            P(("rep", "ep"), None, None),
            P(("rep", "ep"), None, None),
            P(("rep", "ep"), None),
            P(("rep", "ep"), None),
            P(("rep", "ep"), None),
            P(("rep", "ep"), None, None),
            P(("rep", "ep"), None, None),
            P(("rep", "ep"), None),
            P(("rep", "ep"), None),
            P(("rep", "ep")),
        ),
        out_specs=(P(("rep", "ep"), None, None), P(("rep", "ep"), None)),
        check_vma=False,
    )
```
